128 devices in a mesh: group: 2 (over core), tok: 4 (over x), vocab: 16 (over y, z).
Axes of the slice: x: 4, y: 4, z: 4, core: 2. Of those that a mesh axis runs over, the one named last changes fastest.
Arguments:
- teacher_hidden: bfloat16 [8192, 8192], P('tok', ('group', 'vocab')), may hold values from -160 to 160
- student_hidden: bfloat16 [8192, 5120], P('tok', ('group', 'vocab')), may hold values from -160 to 160
- teacher_gain: bfloat16 [8192], P(('group', 'vocab')), may hold values from 0.099609375 to 1.8984375
- student_gain: bfloat16 [5120], P(('group', 'vocab')), may hold values from 0.099609375 to 1.8984375
- teacher_head: bfloat16 [8192, 98304], P(None, ('group', 'tok', 'vocab')), may hold values from -10 to 10
- student_head: bfloat16 [5120, 98304], P(None, ('group', 'tok', 'vocab')), may hold values from -10 to 10
- targets: int32 [8192], replicated, may hold values from 0 to 98303
- mask_positions: int32 [1024], replicated, may hold values from 0 to 2047, as said below
- mask_counts: int32 [4], replicated, may hold values from 1 to 256, as said below
- mask_time: int32 [1], replicated, may hold values from 250 to 1000
Outputs:
- slot_kl: float32 [1024], P('tok')
- slot_nll: float32 [1024], P('tok')
- losses: float32 [2], replicated
The draws below stay inside these ranges and needn't reach their ends.
Inputs may be any that keep to these rules, and one draw needn't show every extreme that they name: `mask_positions`: entries t * 256 to (t + 1) * 256 - 1 are distinct positions within tok shard t's 2048 tokens; only the first mask_counts[t] of them are masked, the others carry no weight. `mask_counts`: one shard has exactly 256; all shards together have exactly 512.
All inputs are finite; a program needn't handle non-finite values.
Results may differ from the reference program's by a relative error of at most 0.00071.
Values may be sent and summed in bfloat16 or wider, within the bound.
A program may use at most 192 MiB of HBM per device.

```python
import math
import jax
import jax.numpy as jnp
from jax import lax

DT = 8192
DS = 5120
TOK_DEV = 2048
M_DEV = 256
TOKENS = 8192
MASK_TOTAL = 512
VOCAB = 98304
N_TOK = 4


def sample_hidden(key, width):
    key_body, key_row, key_column = jax.random.split(key, 3)
    row_scale = jnp.exp(jax.random.uniform(key_row, (TOKENS, 1), minval=0.0, maxval=math.log(10.0)))
    column_scale = jnp.exp(jax.random.uniform(key_column, (1, width), minval=math.log(0.4), maxval=math.log(4.0)))
    values = jnp.clip(jax.random.normal(key_body, (TOKENS, width)), -4.0, 4.0)
    return (values * row_scale * column_scale).astype(jnp.bfloat16)


def head_columns(key, width):
    scale = 3.0 / math.sqrt(width)
    columns = jnp.clip(jax.random.normal(key, (width, VOCAB)), -4.0, 4.0) * scale
    return columns.astype(jnp.bfloat16)


def draw_teacher_hidden(key, part):
    key = jax.random.fold_in(key, 1)
    return sample_hidden(key, DT)


def draw_student_hidden(key, part):
    key = jax.random.fold_in(key, 2)
    return sample_hidden(key, DS)


def draw_teacher_head(key, part):
    key = jax.random.fold_in(key, 3)
    return head_columns(key, DT)


def draw_student_head(key, part):
    key = jax.random.fold_in(key, 4)
    return head_columns(key, DS)


def draw_mask_positions(key, part):
    key = jax.random.fold_in(key, 5)
    shard_total = TOKENS // TOK_DEV
    shard_keys = jax.random.split(key, shard_total)
    listed = jax.vmap(lambda shard_key: jax.random.permutation(shard_key, TOK_DEV)[:M_DEV])(shard_keys)
    return listed.reshape(-1).astype(jnp.int32)


def draw_mask_counts(key, part):
    key = jax.random.fold_in(key, 6)
    key_step, key_order = jax.random.split(key)
    shard_total = TOKENS // TOK_DEV
    others = shard_total - 1
    remaining = M_DEV * (shard_total // 2 - 1)
    base = remaining // others
    extra = remaining - base * others
    halfway = base // 2
    steps = jax.random.randint(key_step, (others,), -halfway, halfway + 1)
    ordinal = jnp.arange(others)
    paired = jnp.where(ordinal % 2 == 0, steps, -jnp.roll(steps, 1))
    paired = jnp.where((ordinal % 2 == 0) & (ordinal + 1 >= others), 0, paired)
    loads = base + paired + jnp.where(ordinal == 0, extra, 0)
    filled = jnp.concatenate([jnp.full((1,), M_DEV, jnp.int32), loads.astype(jnp.int32)])
    shuffle = jax.random.permutation(key_order, shard_total)
    return filled[shuffle].astype(jnp.int32)


def set_ends(values, rng, smallest, top_value):
    index_at = [jax.random.randint(jax.random.fold_in(rng, axis), (), 0, length) for axis, length in enumerate(values.shape)]
    widest = values.shape.index(max(values.shape))
    neighbour = index_at[:widest] + [(index_at[widest] + 1) % values.shape[widest]] + index_at[widest + 1:]
    return values.at[tuple(index_at)].set(smallest).at[tuple(neighbour)].set(top_value)


def setup_inputs(seed: int = 0) -> dict:
    key_of = jax.random.split(jax.random.key(seed), 11)
    return {
        "teacher_hidden": draw_teacher_hidden(jax.random.fold_in(key_of[10], 71), 0),
        "student_hidden": draw_student_hidden(jax.random.fold_in(key_of[10], 71), 0),
        "teacher_gain": jnp.clip(1.0 + 0.18 * jax.random.normal(key_of[2], (DT,), jnp.float32), 0.099609375, 1.8984375).astype(jnp.bfloat16),
        "student_gain": jnp.clip(1.0 + 0.18 * jax.random.normal(key_of[3], (DS,), jnp.float32), 0.099609375, 1.8984375).astype(jnp.bfloat16),
        "teacher_head": draw_teacher_head(jax.random.fold_in(key_of[10], 71), 0),
        "student_head": draw_student_head(jax.random.fold_in(key_of[10], 71), 0),
        "targets": set_ends(jax.random.randint(key_of[6], (TOKENS,), 0, VOCAB), jax.random.fold_in(key_of[6], 1), 0, VOCAB - 1).astype(jnp.int32),
        "mask_positions": draw_mask_positions(jax.random.fold_in(key_of[10], 71), 0),
        "mask_counts": draw_mask_counts(jax.random.fold_in(key_of[10], 71), 0),
        "mask_time": jax.random.randint(key_of[9], (1,), 250, 1001).astype(jnp.int32),
    }


EPS = 1e-06

def normalize(hidden_rows, feature_gain):
    hidden_rows = hidden_rows.astype(jnp.float32)
    mean_square = lax.optimization_barrier(jnp.mean(hidden_rows * hidden_rows, axis=1, keepdims=True))
    scaled = hidden_rows * lax.rsqrt(mean_square + EPS) * feature_gain.astype(jnp.float32)[None, :]
    return scaled.astype(jnp.bfloat16)

def live_order(mask_positions, mask_counts):
    shard_ends = jnp.cumsum(mask_counts).astype(jnp.int32)
    shard_starts = shard_ends - mask_counts
    ordinal = jnp.arange(MASK_TOTAL, dtype=jnp.int32)
    shard_index = lax.optimization_barrier(jnp.sum((ordinal[:, None] >= shard_ends[None, :]).astype(jnp.int32), axis=1)).astype(jnp.int32)
    slot_index = (shard_index * M_DEV + ordinal - shard_starts[shard_index]).astype(jnp.int32)
    token_index = (shard_index * TOK_DEV + mask_positions[slot_index]).astype(jnp.int32)
    return (slot_index, token_index)

def block_terms(stacked, teacher_head, student_head):
    normed_teacher, normed_student, target_ids = stacked
    logit_teacher = jnp.dot(normed_teacher, teacher_head, preferred_element_type=jnp.float32)
    logit_student = jnp.dot(normed_student, student_head, preferred_element_type=jnp.float32)
    lse_teacher = jax.nn.logsumexp(logit_teacher, axis=1)
    lse_student = jax.nn.logsumexp(logit_student, axis=1)
    prob_teacher = jnp.exp(logit_teacher - lse_teacher[:, None])
    row_kl = lax.optimization_barrier(jnp.sum(prob_teacher * (logit_teacher - logit_student), axis=1)) - lse_teacher + lse_student
    picked = jnp.take_along_axis(logit_student, target_ids[:, None], axis=1)[:, 0]
    return (row_kl, lse_student - picked)

def reference(teacher_hidden, student_hidden, teacher_gain, student_gain, teacher_head, student_head, targets, mask_positions, mask_counts, mask_time):
    slot_index, token_index = live_order(mask_positions, mask_counts)
    normed_teacher = normalize(teacher_hidden[token_index], teacher_gain)
    normed_student = normalize(student_hidden[token_index], student_gain)
    target_ids = targets[token_index].astype(jnp.int32)
    block_rows = math.gcd(MASK_TOTAL, 128)
    block_count = MASK_TOTAL // block_rows
    stacked = (normed_teacher.reshape(block_count, block_rows, DT), normed_student.reshape(block_count, block_rows, DS), target_ids.reshape(block_count, block_rows))
    row_kl, row_nll = lax.map(lambda pieces: block_terms(pieces, teacher_head, student_head), stacked)
    row_kl = row_kl.reshape(MASK_TOTAL)
    row_nll = row_nll.reshape(MASK_TOTAL)
    slot_kl = jnp.zeros((N_TOK * M_DEV,), jnp.float32).at[slot_index].set(row_kl)
    slot_nll = jnp.zeros((N_TOK * M_DEV,), jnp.float32).at[slot_index].set(row_nll)
    weight = 1000.0 / mask_time[0].astype(jnp.float32)
    losses = jnp.stack([weight * jnp.sum(row_nll) / TOKENS, jnp.sum(row_kl) / jnp.sum(mask_counts).astype(jnp.float32)])
    return (slot_kl, slot_nll, losses)
```

```python
import functools

import jax
import jax.numpy as jnp
from jax import lax
from jax.experimental import pallas as pl
from jax.experimental.pallas import tpu as pltpu
from jax.sharding import PartitionSpec as P

EPS = 1e-06
MESH = pl.DeviceIdType.MESH
f32 = jnp.float32
bf16 = jnp.bfloat16

ROWS = 512
Q = 128
DT = 8192
DS = 5120
NV = 768
NT = 256
XT = 144

N_ICI = 24
N_SIB = 16


def off(i):
    return jnp.where(i < 2, i, 5 - i)


def body(
    th, sh, tg, sg, wt_hbm, ws_hbm, targets, positions, counts, mask_time,
    out_kl, out_nll, out_loss,
    ht, hs, wt, ws, xa, xb, xc, acc_t, acc_s, tok_col, tgt_col,
    pay, p1, tx, tz, ty, tgp, fx, fy, fz, fg,
    load_sem, p1_s, p1_r, rnd_s, rnd_r, ici_s, ici_r, sib_s, sib_r,
):
    g = lax.axis_index("group")
    x = lax.axis_index("tok")
    v = lax.axis_index("vocab")
    y = v // 4
    z = v % 4
    sib = {"group": 1 - g}

    def at_axis(axis, k):
        if axis == "x":
            return {"tok": (x + k) % 4}
        if axis == "y":
            return {"vocab": ((y + k) % 4) * 4 + z}
        return {"vocab": y * 4 + (z + k) % 4}

    loads = [
        pltpu.make_async_copy(th, ht, load_sem.at[0]),
        pltpu.make_async_copy(sh, hs, load_sem.at[1]),
    ]
    for i in range(4):
        r = pl.ds(i * (DT // 4), DT // 4)
        loads.append(pltpu.make_async_copy(wt_hbm.at[r], wt.at[r], load_sem.at[2 + i]))
        r = pl.ds(i * (DS // 4), DS // 4)
        loads.append(pltpu.make_async_copy(ws_hbm.at[r], ws.at[r], load_sem.at[6 + i]))
    for c in loads:
        c.start()

    barrier = pltpu.get_barrier_semaphore()
    peers = [at_axis(a, k) for a in "xyz" for k in (1, 2, 3)] + [sib]
    for d in peers:
        pl.semaphore_signal(barrier, inc=1, device_id=d, device_id_type=MESH)

    starts = []
    total = jnp.int32(0)
    for t in range(4):
        starts.append(total)
        total = total + counts[t]
    lane256 = lax.broadcasted_iota(jnp.int32, (1, 256), 1)
    pos_rows = []
    for t in range(4):
        p = jnp.concatenate([positions[2 * t : 2 * t + 1, :], positions[2 * t + 1 : 2 * t + 2, :]], axis=1)
        pos_rows.append(jnp.where(lane256 < counts[t], p + 2048 * t, 0))

    def tokens(q, _):
        d = (
            lax.broadcasted_iota(jnp.int32, (Q, 256), 0)
            + q * Q
            - lax.broadcasted_iota(jnp.int32, (Q, 256), 1)
        )
        s = jnp.zeros((Q, 256), jnp.int32)
        for t in range(4):
            s = s + jnp.where(d == starts[t], pos_rows[t], 0)
        tok_col[q] = jnp.sum(s.astype(f32), axis=1, keepdims=True)
        return 0

    lax.fori_loop(0, 4, tokens, 0)
    loads[0].wait()
    loads[1].wait()
    pl.semaphore_wait(barrier, len(peers))

    lane = lax.broadcasted_iota(jnp.int32, (Q, 128), 1)

    def tiny_copy(q, k):
        return pltpu.make_async_remote_copy(
            src_ref=tx.at[4 + q], dst_ref=tx.at[x], send_sem=rnd_s.at[0, k], recv_sem=rnd_r.at[0, k],
            device_id={"tok": q}, device_id_type=MESH)

    def pay_copy(q, k):
        return pltpu.make_async_remote_copy(
            src_ref=pay.at[q], dst_ref=p1.at[x], send_sem=p1_s.at[k], recv_sem=p1_r.at[k],
            device_id={"tok": q}, device_id_type=MESH)

    def pick(k, _):
        q = (x + 1 + jnp.where(k == 1, 2, jnp.where(k == 2, 1, k))) % 4
        tok = tok_col[q].astype(jnp.int32) - 2048 * x
        hot = jnp.where(tok == lax.broadcasted_iota(jnp.int32, (Q, 2048), 1), 1.0, 0.0).astype(bf16)
        ct = jnp.dot(hot, ht[...], preferred_element_type=f32)
        cs = jnp.dot(hot, hs[...], preferred_element_type=f32)
        sq_t = jnp.sum(ct * ct, axis=1, keepdims=True)
        sq_s = jnp.sum(cs * cs, axis=1, keepdims=True)
        rest = jnp.concatenate([cs[:, 128:160], jnp.zeros((Q, 96), f32)], axis=1)
        rest = jnp.where(lane == 32, sq_t, jnp.where(lane == 33, sq_s, rest))
        rest = jnp.transpose(rest)
        tx[4 + q] = rest[32:40]
        pay[q, 0:128] = ct[:, :128].astype(bf16)
        pay[q, 128:256] = ct[:, 128:].astype(bf16)
        pay[q, 256:384] = cs[:, :128].astype(bf16)
        pay[q, 384:416] = rest[:32].astype(bf16)

        @pl.when(k < 3)
        def _():
            tiny_copy(q, k).start()
            pay_copy(q, k).start()

        return 0

    lax.fori_loop(0, 4, pick, 0)

    for k in range(3):
        tiny_copy((x + 1) % 4, k).wait_recv()
    sums = tx[4 + x]
    for k in (1, 2, 3):
        sums = sums + tx[(x + k) % 4]

    def spread(buf, axis, at, number, rnd):
        if axis == "g":
            cps = [pltpu.make_async_remote_copy(
                src_ref=buf.at[at], dst_ref=buf.at[at], send_sem=rnd_s.at[rnd, 0], recv_sem=rnd_r.at[rnd, 0],
                device_id=sib, device_id_type=MESH)]
        else:
            cps = [pltpu.make_async_remote_copy(
                src_ref=buf.at[at], dst_ref=buf.at[at], send_sem=rnd_s.at[rnd, k - 1],
                recv_sem=rnd_r.at[rnd, k - 1], device_id=at_axis(axis, k), device_id_type=MESH)
                for k in (1, 3, 2)]
        for c in cps:
            c.start()
        for c in cps:
            c.wait_recv()
        ends.extend(cps)
        return [buf[i] for i in range(number)]

    ends = []
    for axis, buf, at, number, rnd in (("z", tz, z, 4, 1), ("y", ty, y, 4, 2), ("g", tgp, g, 2, 3)):
        buf[at] = sums
        parts = spread(buf, axis, at, number, rnd)
        sums = parts[0]
        for p in parts[1:]:
            sums = sums + p

    width = jnp.where(lax.broadcasted_iota(jnp.int32, (8, 128), 0) == 0, float(DT), float(DS))
    scale = lax.rsqrt(sums / width + EPS)
    scale_col = jnp.transpose(jnp.concatenate([scale, jnp.zeros((120, 128), f32)], axis=0))
    gain_t = tg[...].astype(f32)
    gain_s = sg[...].astype(f32)
    eye = lax.broadcasted_iota(jnp.int32, (32, 32), 0) == lax.broadcasted_iota(jnp.int32, (32, 32), 1)
    gain_col = jnp.sum(jnp.where(eye, gain_s[:, 128:160], 0.0), axis=1, keepdims=True)
    for k in range(3):
        pay_copy((x + 1) % 4, k).wait_recv()

    def mine(lo, hi):
        s = pay[x, lo:hi].astype(f32)
        for k in (1, 2, 3):
            s = s + p1[(x + k) % 4, lo:hi].astype(f32)
        return s

    xa[g, y, z, x, 0:128] = (mine(0, 128) * scale_col[:, 0:1] * gain_t[:, :128]).astype(bf16)
    xb[g, y, z, x, 0:128] = (mine(128, 256) * scale_col[:, 0:1] * gain_t[:, 128:]).astype(bf16)
    xc[g, y, z, x] = (mine(256, 384) * scale_col[:, 1:2] * gain_s[:, :128]).astype(bf16)
    rest = (mine(384, 416) * scale[1:2] * gain_col).astype(bf16)
    xa[g, y, z, x, 128:144] = rest[:16]
    xb[g, y, z, x, 128:144] = rest[16:]

    order = ("xyz", "yzx", "zxy")
    here = {"x": x, "y": y, "z": z}
    everything = slice(None)

    def box(c, a1, a2, a3):
        if c == 0:
            return xa.at[g, a2, a3, a1]
        if c == 1:
            return xb.at[g, a1, a2, a3]
        return xc.at[g, a3, a1, a2]

    def coords(c):
        return [here[a] for a in order[c]]

    def ici(c, n, ref, axis, k):
        return pltpu.make_async_remote_copy(
            src_ref=ref, dst_ref=ref, send_sem=ici_s.at[c, n], recv_sem=ici_r.at[c, n],
            device_id=at_axis(axis, k), device_id_type=MESH)

    def sibling(c, n, ref):
        return pltpu.make_async_remote_copy(
            src_ref=ref, dst_ref=ref, send_sem=sib_s.at[c, n], recv_sem=sib_r.at[c, n],
            device_id=sib, device_id_type=MESH)

    def first(c, n):
        a1, a2, a3 = coords(c)
        axis = order[c][0]
        cut = 64 if c == 2 else 80
        rows = 128 if c == 2 else XT
        if n == 0:
            return ici(c, 0, box(c, a1, a2, a3), axis, 1)
        if n == 1:
            return ici(c, 1, box(c, a1, a2, a3), axis, 3)
        if n == 2:
            return ici(c, 2, box(c, (a1 + 3) % 4, a2, a3).at[0:cut], axis, 1)
        return ici(c, 3, box(c, (a1 + 1) % 4, a2, a3).at[cut:rows], axis, 3)

    def second(c, n):
        a1, a2, a3 = coords(c)
        axis = order[c][1]
        if n == 0:
            return ici(c, 4, box(c, everything, a2, a3), axis, 1)
        if n == 1:
            return ici(c, 5, box(c, everything, a2, a3), axis, 3)
        if n == 2:
            return ici(c, 6, box(c, pl.ds(0, 2), (a2 + 3) % 4, a3), axis, 1)
        return ici(c, 7, box(c, pl.ds(2, 2), (a2 + 1) % 4, a3), axis, 3)

    def third(c, n, i):
        a1, a2, a3 = coords(c)
        axis = order[c][2]
        b2 = (a2 + off(i)) % 4
        if n == 0:
            return ici(c, 8 + i, box(c, everything, b2, a3), axis, 1)
        if n == 1:
            return ici(c, 12 + i, box(c, everything, b2, a3), axis, 3)
        if n == 2:
            return ici(c, 16 + i, box(c, pl.ds(0, 2), b2, (a3 + 3) % 4), axis, 1)
        return ici(c, 20 + i, box(c, pl.ds(2, 2), b2, (a3 + 1) % 4), axis, 3)

    def across(c, i, k):
        a1, a2, a3 = coords(c)
        return sibling(c, 4 * k + i, box(c, everything, (a2 + off(i)) % 4, (a3 + k) % 4))

    colors = range(3)
    for c in colors:
        first(c, 0).start()
        first(c, 1).start()

    digits = targets[...]
    table = jnp.concatenate(
        [(digits & 255), (digits >> 8) & 255, digits >> 16], axis=1).astype(f32).astype(bf16)
    first_entry = ((g * 4 + x) * 16 + v) * NV

    def find_targets(q, _):
        tok = tok_col[q].astype(jnp.int32)
        hot = jnp.where(
            (tok >> 7) == lax.broadcasted_iota(jnp.int32, (Q, 64), 1), 1.0, 0.0).astype(bf16)
        found = jnp.dot(hot, table, preferred_element_type=f32)
        mixed = found[:, :128] + 256.0 * found[:, 128:256] + 65536.0 * found[:, 256:]
        ids = jnp.sum(jnp.where(lane == (tok & 127), mixed, 0.0), axis=1, keepdims=True)
        tgt_col[q] = ids
        return 0

    lax.fori_loop(0, 4, find_targets, 0)
    acc_t[...] = jnp.zeros_like(acc_t)
    acc_s[...] = jnp.zeros_like(acc_s)

    for c in colors:
        first(c, 0).wait_recv()
        first(c, 2).start()
        first(c, 1).wait_recv()
        first(c, 3).start()
    for c in colors:
        first(c, 2).wait_recv()
        first(c, 3).wait_recv()
        second(c, 0).start()
        second(c, 1).start()
        third(c, 0, 0).start()
        third(c, 1, 0).start()
        across(c, 0, 0).start()
    for c in colors:
        second(c, 0).wait_recv()
        second(c, 2).start()
        second(c, 1).wait_recv()
        second(c, 3).start()
        for i in (1, 2):
            third(c, 0, i).start()
            third(c, 1, i).start()
            across(c, i, 0).start()
    for c in colors:
        second(c, 2).wait_recv()
        second(c, 3).wait_recv()
        third(c, 0, 3).start()
        third(c, 1, 3).start()
        across(c, 3, 0).start()
    for c in loads[2:]:
        c.wait()

    def add(acc, xs, w, rows_of):
        xs = jnp.concatenate(xs, axis=1)

        def one(n, _):
            cols = pl.ds(pl.multiple_of(n * NT, NT), NT)
            ws_ = jnp.concatenate([w[r, cols] for r in rows_of], axis=0)
            acc[:, cols] = acc[:, cols] + jnp.dot(xs, ws_, preferred_element_type=f32)
            return 0

        lax.fori_loop(0, NV // NT, one, 0)

    def chunk(gg, yy, zz):
        return gg * 16 + yy * 4 + zz

    def rows_t(n, odd):
        return pl.ds(pl.multiple_of(n * 256 + 128 * odd, 128), 128)

    def multiply(i, ks):
        y_i = (y + off(i)) % 4
        z_i = (z + off(i)) % 4
        x_i = (x + off(i)) % 4
        both = (0, 1)
        at = [(gg, y_i, (z + k) % 4) for k in ks for gg in both]
        add(acc_t, [xa[gg, yy, zz, :, 0:128].reshape(ROWS, 128) for gg, yy, zz in at],
            wt, [rows_t(chunk(*a), 0) for a in at])
        for k in ks:
            xx = (x + k) % 4
            at = [(gg, yy, z_i) for gg in both for yy in range(4)]
            add(acc_t.at[pl.ds(pl.multiple_of(xx * Q, Q), Q)],
                [xb[gg, yy, zz, xx, 0:128] for gg, yy, zz in at],
                wt, [rows_t(chunk(*a), 1) for a in at])
        at = [(gg, (y + k) % 4, zz) for k in ks for gg in both for zz in range(4)]
        add(acc_s.at[pl.ds(pl.multiple_of(x_i * Q, Q), Q)],
            [xc[gg, yy, zz, x_i] for gg, yy, zz in at],
            ws, [pl.ds(pl.multiple_of(chunk(*a) * 160, 32), 128) for a in at])

    def multiply_rest(i):
        y_i = (y + off(i)) % 4
        z_i = (z + off(i)) % 4
        both = (0, 1)
        at_a = [(gg, y_i, zz) for gg in both for zz in range(4)]
        at_b = [(gg, yy, z_i) for gg in both for yy in range(4)]
        xs = []
        for xx in range(4):
            t = jnp.concatenate(
                [xa[gg, yy, zz, xx, 128:144] for gg, yy, zz in at_a]
                + [xb[gg, yy, zz, xx, 128:144] for gg, yy, zz in at_b], axis=0)
            xs.append(jnp.transpose(t.astype(f32)).astype(bf16))
        rows_of = [pl.ds(pl.multiple_of(chunk(*a) * 160 + 128, 16), 16) for a in at_a]
        rows_of += [pl.ds(pl.multiple_of(chunk(*a) * 160 + 144, 16), 16) for a in at_b]
        add(acc_s, [jnp.concatenate(xs, axis=0)], ws, rows_of)

    def step(i, _):
        for c in colors:
            third(c, 0, i).wait_recv()
            third(c, 2, i).start()
            across(c, i, 3).start()
            third(c, 1, i).wait_recv()
            third(c, 3, i).start()
            across(c, i, 1).start()
        for c in colors:
            for k in (0, 1, 3):
                across(c, i, k).wait_recv()
        multiply(i, (0, 1, 3))
        for c in colors:
            third(c, 2, i).wait_recv()
            third(c, 3, i).wait_recv()
            across(c, i, 2).start()
        for c in colors:
            across(c, i, 2).wait_recv()
        multiply(i, (2,))
        multiply_rest(i)
        return 0

    lax.fori_loop(0, 4, step, 0)

    def stats(q, m):
        r = pl.ds(pl.multiple_of(q * Q, Q), Q)
        lt = acc_t[r, :]
        ls = acc_s[r, :]
        mt = jnp.max(lt, axis=1, keepdims=True)
        ms = jnp.max(ls, axis=1, keepdims=True)
        et = jnp.exp(lt - mt)
        zt = jnp.sum(et, axis=1, keepdims=True)
        dd = jnp.sum(et * (lt - ls), axis=1, keepdims=True)
        zs = jnp.sum(jnp.exp(ls - ms), axis=1, keepdims=True)
        col = tgt_col[q].astype(jnp.int32) - first_entry
        hit = col == lax.broadcasted_iota(jnp.int32, (Q, NV), 1)
        tl = jnp.sum(jnp.where(hit, ls, 0.0), axis=1, keepdims=True)
        for n, val in enumerate((mt + jnp.log(zt), ms + jnp.log(zs), dd / zt, tl)):
            m = jnp.where(lane == 4 * n + q, val, m)
        return m

    m = lax.fori_loop(0, 4, stats, jnp.zeros((Q, 128), f32))
    val = jnp.transpose(m)[:16]

    for axis, buf, at, number, rnd in (("g", fg, g, 2, 4), ("x", fx, x, 4, 5), ("y", fy, y, 4, 6), ("z", fz, z, 4, 7)):
        buf[at] = val
        parts = spread(buf, axis, at, number, rnd)

        def lse(lo):
            top = parts[0][lo : lo + 4]
            for p in parts[1:]:
                top = jnp.maximum(top, p[lo : lo + 4])
            es = [jnp.exp(p[lo : lo + 4] - top) for p in parts]
            tot = es[0]
            for e in es[1:]:
                tot = tot + e
            return top + jnp.log(tot), es, tot

        lse_t, es, tot = lse(0)
        lse_s, _, _ = lse(4)
        cross = es[0] * parts[0][8:12]
        tl = parts[0][12:16]
        for e, p in zip(es[1:], parts[1:]):
            cross = cross + e * p[8:12]
            tl = tl + p[12:16]
        val = jnp.concatenate([lse_t, lse_s, cross / tot, tl], axis=0)

    lse_t, lse_s, cross, tl = (val[4 * n : 4 * n + 4] for n in range(4))
    kl = cross - lse_t + lse_s
    nll = lse_s - tl
    kl_total = jnp.sum(jnp.sum(kl, axis=1, keepdims=True), axis=0, keepdims=True)
    nll_total = jnp.sum(jnp.sum(nll, axis=1, keepdims=True), axis=0, keepdims=True)
    time = jnp.full((1, 1), mask_time[0], jnp.int32).astype(f32)
    masked = jnp.full((1, 1), total, jnp.int32).astype(f32)
    weight = 1000.0 / time
    out_loss[...] = jnp.concatenate([weight * nll_total / 8192.0, kl_total / masked], axis=1)

    cols = jnp.transpose(jnp.concatenate([kl, nll, jnp.zeros((120, 128), f32)], axis=0))
    start = jnp.int32(0)
    count = jnp.int32(0)
    for t in range(4):
        start = start + jnp.where(x == t, starts[t], 0)
        count = count + jnp.where(x == t, counts[t], 0)
    slot = lax.broadcasted_iota(jnp.int32, (Q, 256), 1)
    gap = lax.broadcasted_iota(jnp.int32, (Q, 256), 0) - slot
    for n, out in ((0, out_kl), (4, out_nll)):
        s = jnp.zeros((Q, 256), f32)
        for q in range(4):
            s = s + jnp.where(gap == start - q * Q, cols[:, n + q : n + q + 1], 0.0)
        s = jnp.sum(s, axis=0, keepdims=True)
        out[...] = jnp.where(lane256 < count, s, 0.0)

    for k in range(3):
        tiny_copy((x + 1) % 4, k).wait_send()
        pay_copy((x + 1) % 4, k).wait_send()
    for c in ends:
        c.wait_send()
    for c in colors:
        for n in range(4):
            first(c, n).wait_send()
            second(c, n).wait_send()

    def drain(i, _):
        for c in colors:
            for n in range(4):
                third(c, n, i).wait_send()
                across(c, i, n).wait_send()
        return 0

    lax.fori_loop(0, 4, drain, 0)


def shards(th, sh, tg, sg, wt, ws, targets, positions, counts, mask_time):
    vm = pl.BlockSpec(memory_space=pltpu.VMEM)
    sm = pl.BlockSpec(memory_space=pltpu.SMEM)
    anyspace = pl.BlockSpec(memory_space=pl.ANY)
    dma = pltpu.SemaphoreType.DMA
    kl, nll, loss = pl.pallas_call(
        body,
        out_shape=(
            jax.ShapeDtypeStruct((1, 256), f32),
            jax.ShapeDtypeStruct((1, 256), f32),
            jax.ShapeDtypeStruct((1, 2), f32),
        ),
        in_specs=[anyspace, anyspace, vm, vm, anyspace, anyspace, vm, vm, sm, sm],
        out_specs=(vm, vm, vm),
        scratch_shapes=[
            pltpu.VMEM((2048, 256), bf16),
            pltpu.VMEM((2048, 160), bf16),
            pltpu.VMEM((DT, NV), bf16),
            pltpu.VMEM((DS, NV), bf16),
            pltpu.VMEM((2, 4, 4, 4, XT, 128), bf16),
            pltpu.VMEM((2, 4, 4, 4, XT, 128), bf16),
            pltpu.VMEM((2, 4, 4, 4, 128, 128), bf16),
            pltpu.VMEM((ROWS, NV), f32),
            pltpu.VMEM((ROWS, NV), f32),
            pltpu.VMEM((4, Q, 1), f32),
            pltpu.VMEM((4, Q, 1), f32),
            pltpu.VMEM((4, 416, 128), bf16),
            pltpu.VMEM((4, 416, 128), bf16),
            pltpu.VMEM((8, 8, 128), f32),
            pltpu.VMEM((4, 8, 128), f32),
            pltpu.VMEM((4, 8, 128), f32),
            pltpu.VMEM((2, 8, 128), f32),
            pltpu.VMEM((4, 16, 128), f32),
            pltpu.VMEM((4, 16, 128), f32),
            pltpu.VMEM((4, 16, 128), f32),
            pltpu.VMEM((2, 16, 128), f32),
            dma((10,)),
            dma((3,)),
            dma((3,)),
            dma((8, 3)),
            dma((8, 3)),
            dma((3, N_ICI)),
            dma((3, N_ICI)),
            dma((3, N_SIB)),
            dma((3, N_SIB)),
        ],
        compiler_params=pltpu.CompilerParams(
            collective_id=0, has_side_effects=True, vmem_limit_bytes=58 * 1024 * 1024),
        name="elbo",
    )(
        th, sh, tg.reshape(1, 256), sg.reshape(1, 160), wt, ws,
        targets.reshape(64, 128), positions.reshape(8, 128), counts, mask_time,
    )
    return kl.reshape(256), nll.reshape(256), loss.reshape(2)


def solution(mesh):
    feats = ("group", "vocab")
    cols = ("group", "tok", "vocab")
    in_specs = (
        P("tok", feats), P("tok", feats), P(feats), P(feats),
        P(None, cols), P(None, cols), P(), P(), P(), P(),
    )
    out_specs = (P("tok"), P("tok"), P())
    return jax.shard_map(shards, mesh=mesh, in_specs=in_specs, out_specs=out_specs, check_vma=False)
```

```python
import functools

import jax
import jax.numpy as jnp
from jax import lax
from jax.experimental import pallas as pl
from jax.experimental.pallas import tpu as pltpu
from jax.sharding import PartitionSpec as P

EPS = 1e-06
MESH = pl.DeviceIdType.MESH
f32 = jnp.float32
bf16 = jnp.bfloat16

ROWS = 512
Q = 128
DT = 8192
DS = 5120
NV = 768
NT = 256
XT = 144

N_ICI = 24
N_SIB = 16


def off(i):
    return jnp.where(i < 2, i, 5 - i)


def body(
    th, sh, tg_any, sg, wt_hbm, ws_hbm, targets_any, positions_any, counts,
    out,
    ht, hs, tg, targets, positions, hot, wt, ws, xa, xb, xc, acc_t, acc_s, tok_col, tgt_col,
    sc_t, sc_s, pay_a, pay_b, pay_c, p1a, p1b, p1c, tx, tz, ty, tgp, txx, fx, fy, fz,
    load_sem, p1_s, p1_r, rnd_s, rnd_r, ici_s, ici_r, sib_s, sib_r,
):
    g = lax.axis_index("group")
    x = lax.axis_index("tok")
    v = lax.axis_index("vocab")
    y = v // 4
    z = v % 4
    sib = {"group": 1 - g}

    def at_axis(axis, k):
        if axis == "x":
            return {"tok": (x + k) % 4}
        if axis == "y":
            return {"vocab": ((y + k) % 4) * 4 + z}
        return {"vocab": y * 4 + (z + k) % 4}

    barrier = pltpu.get_barrier_semaphore()
    peers = [at_axis(a, k) for a in "xyz" for k in (1, 2, 3)] + [sib]
    peers += [{"group": 1 - g, "tok": (x + k) % 4} for k in (1, 2, 3)]
    for d in peers:
        pl.semaphore_signal(barrier, inc=1, device_id=d, device_id_type=MESH)

    small = [
        pltpu.make_async_copy(positions_any, positions, load_sem.at[10]),
        pltpu.make_async_copy(tg_any, tg, load_sem.at[11]),
        pltpu.make_async_copy(targets_any, targets, load_sem.at[12]),
    ]
    loads = [
        pltpu.make_async_copy(th, ht, load_sem.at[0]),
        pltpu.make_async_copy(sh, hs, load_sem.at[1]),
    ]
    for i in range(4):
        r = pl.ds(i * (DT // 4), DT // 4)
        loads.append(pltpu.make_async_copy(wt_hbm.at[r], wt.at[r], load_sem.at[2 + i]))
        r = pl.ds(i * (DS // 4), DS // 4)
        loads.append(pltpu.make_async_copy(ws_hbm.at[r], ws.at[r], load_sem.at[6 + i]))
    for c in small + loads:
        c.start()

    starts = []
    total = jnp.int32(0)
    for t in range(4):
        starts.append(total)
        total = total + counts[t]
    lane256 = lax.broadcasted_iota(jnp.int32, (1, 256), 1)
    small[0].wait()
    pos_rows = []
    for t in range(4):
        p = jnp.concatenate([positions[2 * t : 2 * t + 1, :], positions[2 * t + 1 : 2 * t + 2, :]], axis=1)
        pos_rows.append(jnp.where(lane256 < counts[t], p + 2048 * t, 0))

    def tokens(q, _):
        d = (
            lax.broadcasted_iota(jnp.int32, (Q, 256), 0)
            + q * Q
            - lax.broadcasted_iota(jnp.int32, (Q, 256), 1)
        )
        s = jnp.zeros((Q, 256), jnp.int32)
        for t in range(4):
            s = s + jnp.where(d == starts[t], pos_rows[t], 0)
        tok_col[q] = jnp.sum(s.astype(f32), axis=1, keepdims=True)
        return 0

    lax.fori_loop(0, 4, tokens, 0)

    lane = lax.broadcasted_iota(jnp.int32, (Q, 128), 1)

    def tiny_copy(q, k):
        return pltpu.make_async_remote_copy(
            src_ref=tx.at[4 + q], dst_ref=tx.at[x], send_sem=rnd_s.at[0, k], recv_sem=rnd_r.at[0, k],
            device_id={"tok": q}, device_id_type=MESH)

    pays = ((pay_a, p1a), (pay_b, p1b), (pay_c, p1c))

    def pay_copy(c, q, k):
        src, dst = pays[c]
        return pltpu.make_async_remote_copy(
            src_ref=src.at[q], dst_ref=dst.at[x], send_sem=p1_s.at[c, k], recv_sem=p1_r.at[c, k],
            device_id={"tok": q}, device_id_type=MESH)

    def to(k):
        return (x + 1 + jnp.where(k == 1, 2, jnp.where(k == 2, 1, k))) % 4

    def make_hot(q, _):
        tok = tok_col[q].astype(jnp.int32) - 2048 * x
        hot[pl.ds(pl.multiple_of(q * Q, Q), Q), :] = jnp.where(
            tok == lax.broadcasted_iota(jnp.int32, (Q, 2048), 1), 1.0, 0.0).astype(bf16)
        return 0

    lax.fori_loop(0, 4, make_hot, 0)
    loads[0].wait()
    ct = jnp.dot(hot[...], ht[...], preferred_element_type=f32)
    for q in range(4):
        cq = ct[q * Q : (q + 1) * Q]
        sc_t[q] = jnp.sum(cq * cq, axis=1, keepdims=True)
        pay_a[q] = cq[:, :128].astype(bf16)
        pay_b[q] = cq[:, 128:].astype(bf16)
    pl.semaphore_wait(barrier, len(peers))
    for k in range(3):
        pay_copy(1, to(k), k).start()
    loads[1].wait()
    cs = lax.dot_general(hot[...], hs[...], (((1,), (1,)), ((), ())), preferred_element_type=f32)
    for q in range(4):
        cq = cs[q * Q : (q + 1) * Q]
        sq_s = jnp.sum(cq * cq, axis=1, keepdims=True)
        rest = jnp.concatenate([cq[:, 128:160], jnp.zeros((Q, 96), f32)], axis=1)
        rest = jnp.where(lane == 32, sc_t[q], jnp.where(lane == 33, sq_s, rest))
        rest = jnp.transpose(rest)
        tx[4 + q] = rest[32:40]
        pay_c[q, 0:128] = cq[:, :128].astype(bf16)
        pay_c[q, 128:160] = rest[:32].astype(bf16)
    for k in range(3):
        pay_copy(2, to(k), k).start()
    for k in range(3):
        tiny_copy(to(k), k).start()
    for k in range(3):
        pay_copy(0, to(k), k).start()

    ends = []

    def spread(buf, axis, at, number, rnd, value):
        buf[at] = value
        if axis == "gx":
            devs = [sib] + [at_axis("x", k) for k in (1, 3, 2)]
            devs += [{"group": 1 - g, "tok": (x + k) % 4} for k in (1, 3, 2)]
            cps = [pltpu.make_async_remote_copy(
                src_ref=buf.at[at], dst_ref=buf.at[at], send_sem=rnd_s.at[rnd, n], recv_sem=rnd_r.at[rnd, n],
                device_id=d, device_id_type=MESH) for n, d in enumerate(devs)]
        elif axis == "g":
            cps = [pltpu.make_async_remote_copy(
                src_ref=buf.at[at], dst_ref=buf.at[at], send_sem=rnd_s.at[rnd, 0], recv_sem=rnd_r.at[rnd, 0],
                device_id=sib, device_id_type=MESH)]
        else:
            cps = [pltpu.make_async_remote_copy(
                src_ref=buf.at[at], dst_ref=buf.at[at], send_sem=rnd_s.at[rnd, k - 1],
                recv_sem=rnd_r.at[rnd, k - 1], device_id=at_axis(axis, k), device_id_type=MESH)
                for k in (1, 3, 2)]
        for c in cps:
            c.start()
        ends.extend(cps)

        def finish():
            for c in cps:
                c.wait_recv()
            return [buf[i] for i in range(number)]

        return finish

    def add_up(parts):
        total = parts[0]
        for p in parts[1:]:
            total = total + p
        return total

    def sums_x():
        for k in range(3):
            tiny_copy((x + 1) % 4, k).wait_recv()
        return add_up([tx[4 + x]] + [tx[(x + k) % 4] for k in (1, 2, 3)])

    small[1].wait()
    gain_t = tg[...].astype(f32)
    gain_s = sg[...].astype(f32).reshape(1, 160)
    eye = lax.broadcasted_iota(jnp.int32, (32, 32), 0) == lax.broadcasted_iota(jnp.int32, (32, 32), 1)
    gain_col = jnp.sum(jnp.where(eye, gain_s[:, 128:160], 0.0), axis=1, keepdims=True)

    def mine(c, lo, hi):
        own, others = pays[c]
        s = own[x, lo:hi].astype(f32)
        for k in (1, 2, 3):
            s = s + others[(x + k) % 4, lo:hi].astype(f32)
        return s

    def place(c):
        for k in range(3):
            pay_copy(c, to(k), k).wait_recv()
        if c == 0:
            xa[g, y, z, x, 0:128] = (mine(0, 0, 128) * gain_t[0:1]).astype(bf16)
        elif c == 1:
            xb[g, y, z, x] = (mine(1, 0, 128) * gain_t[1:2]).astype(bf16)
        else:
            xc[g, y, z, x, 0:128] = (mine(2, 0, 128) * gain_s[:, :128]).astype(bf16)
            rest = (mine(2, 128, 160) * gain_col).astype(bf16)
            xa[g, y, z, x, 128:144] = rest[:16]
            xc[g, y, z, x, 128:144] = rest[16:]

    order = ("xyz", "yzx", "zxy")
    here = {"x": x, "y": y, "z": z}
    everything = slice(None)

    def box(c, a1, a2, a3):
        if c == 0:
            return xa.at[g, a2, a3, a1]
        if c == 1:
            return xb.at[g, a1, a2, a3]
        return xc.at[g, a3, a1, a2]

    def coords(c):
        return [here[a] for a in order[c]]

    def ici(c, n, ref, axis, k):
        return pltpu.make_async_remote_copy(
            src_ref=ref, dst_ref=ref, send_sem=ici_s.at[c, n], recv_sem=ici_r.at[c, n],
            device_id=at_axis(axis, k), device_id_type=MESH)

    def sibling(c, n, ref):
        return pltpu.make_async_remote_copy(
            src_ref=ref, dst_ref=ref, send_sem=sib_s.at[c, n], recv_sem=sib_r.at[c, n],
            device_id=sib, device_id_type=MESH)

    def first(c, n):
        return ici(c, n, box(c, *coords(c)), order[c][0], (1, 3, 2)[n])

    def second(c, n):
        a1, a2, a3 = coords(c)
        axis = order[c][1]
        if n == 0:
            return ici(c, 4, box(c, everything, a2, a3), axis, 1)
        if n == 1:
            return ici(c, 5, box(c, everything, a2, a3), axis, 3)
        if n == 2:
            return ici(c, 6, box(c, pl.ds(0, 2), (a2 + 3) % 4, a3), axis, 1)
        return ici(c, 7, box(c, pl.ds(2, 2), (a2 + 1) % 4, a3), axis, 3)

    def third(c, n, i):
        a1, a2, a3 = coords(c)
        axis = order[c][2]
        b2 = (a2 + off(i)) % 4
        if n == 0:
            return ici(c, 8 + i, box(c, everything, b2, a3), axis, 1)
        if n == 1:
            return ici(c, 12 + i, box(c, everything, b2, a3), axis, 3)
        if n == 2:
            return ici(c, 16 + i, box(c, pl.ds(0, 2), b2, (a3 + 3) % 4), axis, 1)
        return ici(c, 20 + i, box(c, pl.ds(2, 2), b2, (a3 + 1) % 4), axis, 3)

    def across(c, i, k):
        a1, a2, a3 = coords(c)
        return sibling(c, 4 * k + i, box(c, everything, (a2 + off(i)) % 4, (a3 + k) % 4))

    colors = (1, 2, 0)
    for c in colors:
        place(c)
        for n in range(3):
            first(c, n).start()
    finish = spread(tz, "z", z, 4, 1, sums_x())

    small[2].wait()
    digits = targets[...]
    table = jnp.concatenate(
        [(digits & 255), (digits >> 8) & 255, digits >> 16], axis=1).astype(f32).astype(bf16)
    first_entry = ((g * 4 + x) * 16 + v) * NV

    def find_targets(q, _):
        tok = tok_col[q].astype(jnp.int32)
        hot = jnp.where(
            (tok >> 7) == lax.broadcasted_iota(jnp.int32, (Q, 64), 1), 1.0, 0.0).astype(bf16)
        found = jnp.dot(hot, table, preferred_element_type=f32)
        mixed = found[:, :128] + 256.0 * found[:, 128:256] + 65536.0 * found[:, 256:]
        ids = jnp.sum(jnp.where(lane == (tok & 127), mixed, 0.0), axis=1, keepdims=True)
        tgt_col[q] = ids
        return 0

    lax.fori_loop(0, 4, find_targets, 0)
    acc_t[...] = jnp.zeros_like(acc_t)
    acc_s[...] = jnp.zeros_like(acc_s)

    for c in colors:
        for n in range(3):
            first(c, n).wait_recv()
        second(c, 0).start()
        second(c, 1).start()
    for c in colors:
        third(c, 0, 0).start()
        third(c, 1, 0).start()
        across(c, 0, 0).start()
    finish = spread(ty, "y", y, 4, 2, add_up(finish()))
    for c in colors:
        second(c, 0).wait_recv()
        second(c, 2).start()
        second(c, 1).wait_recv()
        second(c, 3).start()
    for c in colors:
        for i in (1, 2):
            third(c, 0, i).start()
            third(c, 1, i).start()
            across(c, i, 0).start()
    finish = spread(tgp, "g", g, 2, 3, add_up(finish()))
    for c in loads[2:]:
        c.wait()
    for c in colors:
        second(c, 2).wait_recv()
        second(c, 3).wait_recv()
        third(c, 0, 3).start()
        third(c, 1, 3).start()
        across(c, 3, 0).start()
    finish = spread(txx, "x", x, 4, 8, add_up(finish()))

    def add(acc, xs, w, rows_of):
        xs = jnp.concatenate(xs, axis=1)

        ws_ = jnp.concatenate([w[r, :] for r in rows_of], axis=0)
        acc[...] = acc[...] + jnp.dot(xs, ws_, preferred_element_type=f32)

    def chunk(gg, yy, zz):
        return gg * 16 + yy * 4 + zz

    def rows_t(n, odd):
        return pl.ds(pl.multiple_of(n * 256 + 128 * odd, 128), 128)

    def multiply(i, ks):
        y_i = (y + off(i)) % 4
        z_i = (z + off(i)) % 4
        x_i = (x + off(i)) % 4
        both = (0, 1)
        at = [(gg, y_i, (z + k) % 4) for k in ks for gg in both]
        add(acc_t, [xa[gg, yy, zz, :, 0:128].reshape(ROWS, 128) for gg, yy, zz in at],
            wt, [rows_t(chunk(*a), 0) for a in at])
        for k in ks:
            xx = (x + k) % 4
            at = [(gg, yy, z_i) for gg in both for yy in range(4)]
            add(acc_t.at[pl.ds(pl.multiple_of(xx * Q, Q), Q)],
                [xb[gg, yy, zz, xx] for gg, yy, zz in at],
                wt, [rows_t(chunk(*a), 1) for a in at])
        at = [(gg, (y + k) % 4, zz) for k in ks for gg in both for zz in range(4)]
        add(acc_s.at[pl.ds(pl.multiple_of(x_i * Q, Q), Q)],
            [xc[gg, yy, zz, x_i, 0:128] for gg, yy, zz in at],
            ws, [pl.ds(pl.multiple_of(chunk(*a) * 160, 32), 128) for a in at])

    def multiply_rest(i):
        y_i = (y + off(i)) % 4
        x_i = (x + off(i)) % 4
        at = [(gg, y_i, zz) for gg in (0, 1) for zz in range(4)]
        xs = []
        for xx in range(4):
            t = jnp.concatenate([xa[gg, yy, zz, xx, 128:144] for gg, yy, zz in at], axis=0)
            xs.append(jnp.transpose(t.astype(f32)).astype(bf16))
        add(acc_s, [jnp.concatenate(xs, axis=0)], ws,
            [pl.ds(pl.multiple_of(chunk(*a) * 160 + 128, 16), 16) for a in at])
        xs = []
        rows_of = []
        for gg in (0, 1):
            for yp in (0, 2):
                at = [(gg, yy, zz) for yy in (yp, yp + 1) for zz in range(4)]
                t = jnp.concatenate([xc[gg, yy, zz, x_i, 128:144] for gg, yy, zz in at], axis=0)
                xs.append(jnp.transpose(t.astype(f32)).astype(bf16))
                rows_of += [pl.ds(pl.multiple_of(chunk(*a) * 160 + 144, 16), 16) for a in at]
        add(acc_s.at[pl.ds(pl.multiple_of(x_i * Q, Q), Q)], xs, ws, rows_of)

    def step(i, _):
        def opposite(j):
            for c in colors:
                third(c, 2, j).wait_recv()
                third(c, 3, j).wait_recv()
                across(c, j, 2).start()

        @pl.when(i < 4)
        def _():
            for c in colors:
                third(c, 0, i).wait_recv()
                third(c, 2, i).start()
                third(c, 1, i).wait_recv()
                third(c, 3, i).start()
                across(c, i, 3).start()
                across(c, i, 1).start()
            for c in colors:
                across(c, i, 0).wait_recv()
            multiply(i, (0,))

        @pl.when((i > 0) & (i < 4))
        def _():
            opposite(i - 1)

        @pl.when((i > 0) & (i < 5))
        def _():
            for c in colors:
                for k in (1, 3):
                    across(c, i - 1, k).wait_recv()
            multiply(i - 1, (1, 3))

        @pl.when(i > 1)
        def _():
            for c in colors:
                across(c, i - 2, 2).wait_recv()
            multiply(i - 2, (2,))
            multiply_rest(i - 2)

        @pl.when(i == 4)
        def _():
            opposite(3)

        return 0

    lax.fori_loop(0, 6, step, 0)

    parts = finish()
    width = jnp.where(lax.broadcasted_iota(jnp.int32, (8, 128), 0) % 2 == 0, float(DT), float(DS))
    scale = lax.rsqrt(jnp.concatenate([p[0:2] for p in parts], axis=0) / width + EPS)
    scale = jnp.transpose(jnp.concatenate([scale, jnp.zeros((120, 128), f32)], axis=0))
    for q in range(4):
        sc_t[q] = scale[:, 2 * q : 2 * q + 1]
        sc_s[q] = scale[:, 2 * q + 1 : 2 * q + 2]

    def stats(q, m):
        r = pl.ds(pl.multiple_of(q * Q, Q), Q)
        lt = acc_t[r, :] * sc_t[q]
        ls = acc_s[r, :] * sc_s[q]
        mt = jnp.max(lt, axis=1, keepdims=True)
        ms = jnp.max(ls, axis=1, keepdims=True)
        et = jnp.exp(lt - mt)
        zt = jnp.sum(et, axis=1, keepdims=True)
        dd = jnp.sum(et * (lt - ls), axis=1, keepdims=True)
        zs = jnp.sum(jnp.exp(ls - ms), axis=1, keepdims=True)
        col = tgt_col[q].astype(jnp.int32) - first_entry
        hit = col == lax.broadcasted_iota(jnp.int32, (Q, NV), 1)
        tl = jnp.sum(jnp.where(hit, ls, 0.0), axis=1, keepdims=True)
        for n, val in enumerate((mt + jnp.log(zt), ms + jnp.log(zs), dd / zt, tl)):
            m = jnp.where(lane == 4 * n + q, val, m)
        return m

    m = lax.fori_loop(0, 4, stats, jnp.zeros((Q, 128), f32))
    val = jnp.transpose(m)[:16]

    for axis, buf, at, number, rnd in (("gx", fx, 4 * g + x, 8, 4), ("y", fy, y, 4, 6), ("z", fz, z, 4, 7)):
        parts = spread(buf, axis, at, number, rnd, val)()

        def lse(lo):
            top = parts[0][lo : lo + 4]
            for p in parts[1:]:
                top = jnp.maximum(top, p[lo : lo + 4])
            es = [jnp.exp(p[lo : lo + 4] - top) for p in parts]
            tot = es[0]
            for e in es[1:]:
                tot = tot + e
            return top + jnp.log(tot), es, tot

        lse_t, es, tot = lse(0)
        lse_s, _, _ = lse(4)
        cross = es[0] * parts[0][8:12]
        tl = parts[0][12:16]
        for e, p in zip(es[1:], parts[1:]):
            cross = cross + e * p[8:12]
            tl = tl + p[12:16]
        val = jnp.concatenate([lse_t, lse_s, cross / tot, tl], axis=0)

    out[...] = val

    for k in range(3):
        tiny_copy((x + 1) % 4, k).wait_send()
        for c in colors:
            pay_copy(c, to(k), k).wait_send()
    for c in ends:
        c.wait_send()
    for c in colors:
        for n in range(3):
            first(c, n).wait_send()
        for n in range(4):
            second(c, n).wait_send()

    def drain(i, _):
        for c in colors:
            for n in range(4):
                third(c, n, i).wait_send()
                across(c, i, n).wait_send()
        return 0

    lax.fori_loop(0, 4, drain, 0)


def outputs(val_ref, counts, mask_time, out_kl, out_nll, out_loss):
    x = lax.axis_index("tok")
    lane256 = lax.broadcasted_iota(jnp.int32, (1, 256), 1)
    starts = []
    total = jnp.int32(0)
    for t in range(4):
        starts.append(total)
        total = total + counts[t]
    val = val_ref[...]
    lse_t, lse_s, cross, tl = (val[4 * n : 4 * n + 4] for n in range(4))
    kl = cross - lse_t + lse_s
    nll = lse_s - tl
    kl_total = jnp.sum(jnp.sum(kl, axis=1, keepdims=True), axis=0, keepdims=True)
    nll_total = jnp.sum(jnp.sum(nll, axis=1, keepdims=True), axis=0, keepdims=True)
    time = jnp.full((1, 1), mask_time[0], jnp.int32).astype(f32)
    masked = jnp.full((1, 1), total, jnp.int32).astype(f32)
    weight = 1000.0 / time
    out_loss[...] = jnp.concatenate([weight * nll_total / 8192.0, kl_total / masked], axis=1)

    cols = jnp.transpose(jnp.concatenate([kl, nll, jnp.zeros((120, 128), f32)], axis=0))
    start = jnp.int32(0)
    count = jnp.int32(0)
    for t in range(4):
        start = start + jnp.where(x == t, starts[t], 0)
        count = count + jnp.where(x == t, counts[t], 0)
    slot = lax.broadcasted_iota(jnp.int32, (Q, 256), 1)
    gap = lax.broadcasted_iota(jnp.int32, (Q, 256), 0) - slot
    for n, out in ((0, out_kl), (4, out_nll)):
        s = jnp.zeros((Q, 256), f32)
        for q in range(4):
            s = s + jnp.where(gap == start - q * Q, cols[:, n + q : n + q + 1], 0.0)
        s = jnp.sum(s, axis=0, keepdims=True)
        out[...] = jnp.where(lane256 < count, s, 0.0)


def shards(th, sh, tg, sg, wt, ws, targets, positions, counts, mask_time):
    vm = pl.BlockSpec(memory_space=pltpu.VMEM)
    sm = pl.BlockSpec(memory_space=pltpu.SMEM)
    anyspace = pl.BlockSpec(memory_space=pl.ANY)
    dma = pltpu.SemaphoreType.DMA
    val = pl.pallas_call(
        body,
        out_shape=jax.ShapeDtypeStruct((16, 128), f32),
        in_specs=[anyspace, anyspace, anyspace, vm, anyspace, anyspace, anyspace, anyspace, sm],
        out_specs=vm,
        scratch_shapes=[
            pltpu.VMEM((2048, 256), bf16),
            pltpu.VMEM((160, 2048), bf16),
            pltpu.VMEM((2, 128), bf16),
            pltpu.VMEM((64, 128), jnp.int32),
            pltpu.VMEM((8, 128), jnp.int32),
            pltpu.VMEM((ROWS, 2048), bf16),
            pltpu.VMEM((DT, NV), bf16),
            pltpu.VMEM((DS, NV), bf16),
            pltpu.VMEM((2, 4, 4, 4, XT, 128), bf16),
            pltpu.VMEM((2, 4, 4, 4, 128, 128), bf16),
            pltpu.VMEM((2, 4, 4, 4, XT, 128), bf16),
            pltpu.VMEM((ROWS, NV), f32),
            pltpu.VMEM((ROWS, NV), f32),
            pltpu.VMEM((4, Q, 1), f32),
            pltpu.VMEM((4, Q, 1), f32),
            pltpu.VMEM((4, Q, 1), f32),
            pltpu.VMEM((4, Q, 1), f32),
            pltpu.VMEM((4, 128, 128), bf16),
            pltpu.VMEM((4, 128, 128), bf16),
            pltpu.VMEM((4, 160, 128), bf16),
            pltpu.VMEM((4, 128, 128), bf16),
            pltpu.VMEM((4, 128, 128), bf16),
            pltpu.VMEM((4, 160, 128), bf16),
            pltpu.VMEM((8, 8, 128), f32),
            pltpu.VMEM((4, 8, 128), f32),
            pltpu.VMEM((4, 8, 128), f32),
            pltpu.VMEM((2, 8, 128), f32),
            pltpu.VMEM((4, 8, 128), f32),
            pltpu.VMEM((8, 16, 128), f32),
            pltpu.VMEM((4, 16, 128), f32),
            pltpu.VMEM((4, 16, 128), f32),
            dma((13,)),
            dma((3, 3)),
            dma((3, 3)),
            dma((9, 7)),
            dma((9, 7)),
            dma((3, N_ICI)),
            dma((3, N_ICI)),
            dma((3, N_SIB)),
            dma((3, N_SIB)),
        ],
        compiler_params=pltpu.CompilerParams(
            collective_id=0, has_side_effects=True, vmem_limit_bytes=58 * 1024 * 1024),
        name="elbo",
    )(
        th, sh.T, tg.reshape(2, 128), sg, wt, ws,
        targets.reshape(64, 128), positions.reshape(8, 128), counts,
    )
    kl, nll, loss = pl.pallas_call(
        outputs,
        out_shape=(
            jax.ShapeDtypeStruct((1, 256), f32),
            jax.ShapeDtypeStruct((1, 256), f32),
            jax.ShapeDtypeStruct((1, 2), f32),
        ),
        in_specs=[vm, sm, sm],
        out_specs=(vm, vm, vm),
        name="slots",
    )(val, counts, mask_time)
    return kl.reshape(256), nll.reshape(256), loss.reshape(2)


def solution(mesh):
    feats = ("group", "vocab")
    cols = ("group", "tok", "vocab")
    in_specs = (
        P("tok", feats), P("tok", feats), P(feats), P(feats),
        P(None, cols), P(None, cols), P(), P(), P(), P(),
    )
    out_specs = (P("tok"), P("tok"), P())
    return jax.shard_map(shards, mesh=mesh, in_specs=in_specs, out_specs=out_specs, check_vma=False)
```

```python
import functools

import jax
import jax.numpy as jnp
from jax import lax
from jax.experimental import pallas as pl
from jax.experimental.pallas import tpu as pltpu
from jax.sharding import PartitionSpec as P

EPS = 1e-06
MESH = pl.DeviceIdType.MESH
f32 = jnp.float32
bf16 = jnp.bfloat16

ROWS = 512
Q = 128
DT = 8192
DS = 5120
NV = 768
NT = 256
XT = 144

N_ICI = 24
N_SIB = 16


def off(i):
    return jnp.where(i < 2, i, 5 - i)


def body(
    th, sh, tg_any, sg, wt_hbm, ws_hbm, targets_any, positions_any, counts,
    out,
    ht, hs, tg, targets, positions, hot, wt, ws, xa, xb, xc, acc_t, acc_s, tok_col, tgt_col,
    sc_t, sc_s, pay_a, pay_b, pay_c, p1a, p1b, p1c, tx, tz, ty, tgp, txx, fx, fy,
    load_sem, p1_s, p1_r, rnd_s, rnd_r, ici_s, ici_r, sib_s, sib_r,
):
    g = lax.axis_index("group")
    x = lax.axis_index("tok")
    v = lax.axis_index("vocab")
    y = v // 4
    z = v % 4
    sib = {"group": 1 - g}

    def at_axis(axis, k):
        if axis == "x":
            return {"tok": (x + k) % 4}
        if axis == "y":
            return {"vocab": ((y + k) % 4) * 4 + z}
        return {"vocab": y * 4 + (z + k) % 4}

    def at_plane(k):
        return {"vocab": ((y + k // 4) % 4) * 4 + (z + k % 4) % 4}

    barrier = pltpu.get_barrier_semaphore()
    peers = [at_axis("x", k) for k in (1, 2, 3)] + [at_plane(k) for k in range(1, 16)] + [sib]
    peers += [{"group": 1 - g, "tok": (x + k) % 4} for k in (1, 2, 3)]
    for d in peers:
        pl.semaphore_signal(barrier, inc=1, device_id=d, device_id_type=MESH)

    small = [
        pltpu.make_async_copy(positions_any, positions, load_sem.at[10]),
        pltpu.make_async_copy(tg_any, tg, load_sem.at[11]),
        pltpu.make_async_copy(targets_any, targets, load_sem.at[12]),
    ]
    loads = [
        pltpu.make_async_copy(th, ht, load_sem.at[0]),
        pltpu.make_async_copy(sh, hs, load_sem.at[1]),
    ]
    for i in range(4):
        r = pl.ds(i * (DT // 4), DT // 4)
        loads.append(pltpu.make_async_copy(wt_hbm.at[r], wt.at[r], load_sem.at[2 + i]))
        r = pl.ds(i * (DS // 4), DS // 4)
        loads.append(pltpu.make_async_copy(ws_hbm.at[r], ws.at[r], load_sem.at[6 + i]))
    for c in small + loads:
        c.start()

    starts = []
    total = jnp.int32(0)
    for t in range(4):
        starts.append(total)
        total = total + counts[t]
    lane256 = lax.broadcasted_iota(jnp.int32, (1, 256), 1)
    small[0].wait()
    pos_rows = []
    for t in range(4):
        p = jnp.concatenate([positions[2 * t : 2 * t + 1, :], positions[2 * t + 1 : 2 * t + 2, :]], axis=1)
        pos_rows.append(jnp.where(lane256 < counts[t], p + 2048 * t, 0))

    def tokens(q, _):
        d = (
            lax.broadcasted_iota(jnp.int32, (Q, 256), 0)
            + q * Q
            - lax.broadcasted_iota(jnp.int32, (Q, 256), 1)
        )
        s = jnp.zeros((Q, 256), jnp.int32)
        for t in range(4):
            s = s + jnp.where(d == starts[t], pos_rows[t], 0)
        tok_col[q] = jnp.sum(s.astype(f32), axis=1, keepdims=True)
        return 0

    lax.fori_loop(0, 4, tokens, 0)

    lane = lax.broadcasted_iota(jnp.int32, (Q, 128), 1)

    def tiny_copy(q, k):
        return pltpu.make_async_remote_copy(
            src_ref=tx.at[4 + q], dst_ref=tx.at[x], send_sem=rnd_s.at[0], recv_sem=rnd_r.at[k],
            device_id={"tok": q}, device_id_type=MESH)

    pays = ((pay_a, p1a), (pay_b, p1b), (pay_c, p1c))

    def pay_copy(c, q, k):
        src, dst = pays[c]
        return pltpu.make_async_remote_copy(
            src_ref=src.at[q], dst_ref=dst.at[x], send_sem=p1_s.at[c], recv_sem=p1_r.at[c, k],
            device_id={"tok": q}, device_id_type=MESH)

    def to(k):
        return (x + 1 + jnp.where(k == 1, 2, jnp.where(k == 2, 1, k))) % 4

    def make_hot(q, _):
        tok = tok_col[q].astype(jnp.int32) - 2048 * x
        hot[pl.ds(pl.multiple_of(q * Q, Q), Q), :] = jnp.where(
            tok == lax.broadcasted_iota(jnp.int32, (Q, 2048), 1), 1.0, 0.0).astype(bf16)
        return 0

    lax.fori_loop(0, 4, make_hot, 0)
    loads[0].wait()
    ct = jnp.dot(hot[...], ht[...], preferred_element_type=f32)
    for q in range(4):
        cq = ct[q * Q : (q + 1) * Q]
        sc_t[q] = jnp.sum(cq * cq, axis=1, keepdims=True)
        pay_a[q] = cq[:, :128].astype(bf16)
        pay_b[q] = cq[:, 128:].astype(bf16)
    pl.semaphore_wait(barrier, len(peers))
    for k in range(3):
        pay_copy(1, to(k), k).start()
    loads[1].wait()
    cs = lax.dot_general(hot[...], hs[...], (((1,), (1,)), ((), ())), preferred_element_type=f32)
    for q in range(4):
        cq = cs[q * Q : (q + 1) * Q]
        sq_s = jnp.sum(cq * cq, axis=1, keepdims=True)
        rest = jnp.concatenate([cq[:, 128:160], jnp.zeros((Q, 96), f32)], axis=1)
        rest = jnp.where(lane == 32, sc_t[q], jnp.where(lane == 33, sq_s, rest))
        rest = jnp.transpose(rest)
        tx[4 + q] = rest[32:40]
        pay_c[q, 0:128] = cq[:, :128].astype(bf16)
        pay_c[q, 128:160] = rest[:32].astype(bf16)
    for k in range(3):
        pay_copy(2, to(k), k).start()
    for k in range(3):
        tiny_copy(to(k), k).start()
    for k in range(3):
        pay_copy(0, to(k), k).start()

    ends = []

    used = [3]

    def spread(buf, axis, at, number, rnd, value):
        buf[at] = value
        if axis == "g":
            devs = [sib]
        elif axis == "gx":
            devs = [sib] + [at_axis("x", k) for k in (1, 3, 2)]
            devs += [{"group": 1 - g, "tok": (x + k) % 4} for k in (1, 3, 2)]
        elif axis == "yz":
            devs = [at_plane(k) for k in range(1, 16)]
        else:
            devs = [at_axis(axis, k) for k in (1, 3, 2)]
        cps = [pltpu.make_async_remote_copy(
            src_ref=buf.at[at], dst_ref=buf.at[at], send_sem=rnd_s.at[rnd], recv_sem=rnd_r.at[used[0] + n],
            device_id=d, device_id_type=MESH) for n, d in enumerate(devs)]
        used[0] += len(devs)
        for c in cps:
            c.start()
        ends.append((buf.at[0 : len(devs)], rnd_s.at[rnd]))

        def finish():
            for c in cps:
                c.wait_recv()
            return [buf[i] for i in range(number)]

        return finish

    def add_up(parts):
        total = parts[0]
        for p in parts[1:]:
            total = total + p
        return total

    def sums_x():
        for k in range(3):
            tiny_copy((x + 1) % 4, k).wait_recv()
        return add_up([tx[4 + x]] + [tx[(x + k) % 4] for k in (1, 2, 3)])

    small[1].wait()
    gain_t = tg[...].astype(f32)
    gain_s = sg[...].astype(f32).reshape(1, 160)
    eye = lax.broadcasted_iota(jnp.int32, (32, 32), 0) == lax.broadcasted_iota(jnp.int32, (32, 32), 1)
    gain_col = jnp.sum(jnp.where(eye, gain_s[:, 128:160], 0.0), axis=1, keepdims=True)

    def mine(c, lo, hi):
        own, others = pays[c]
        s = own[x, lo:hi].astype(f32)
        for k in (1, 2, 3):
            s = s + others[(x + k) % 4, lo:hi].astype(f32)
        return s

    def place(c):
        for k in range(3):
            pay_copy(c, to(k), k).wait_recv()
        if c == 0:
            xa[g, y, z, x, 0:128] = (mine(0, 0, 128) * gain_t[0:1]).astype(bf16)
        elif c == 1:
            xb[g, y, z, x] = (mine(1, 0, 128) * gain_t[1:2]).astype(bf16)
        else:
            xc[g, y, z, x, 0:128] = (mine(2, 0, 128) * gain_s[:, :128]).astype(bf16)
            rest = (mine(2, 128, 160) * gain_col).astype(bf16)
            xa[g, y, z, x, 128:144] = rest[:16]
            xc[g, y, z, x, 128:144] = rest[16:]

    order = ("xyz", "yzx", "zxy")
    here = {"x": x, "y": y, "z": z}
    everything = slice(None)

    def box(c, a1, a2, a3):
        if c == 0:
            return xa.at[g, a2, a3, a1]
        if c == 1:
            return xb.at[g, a1, a2, a3]
        return xc.at[g, a3, a1, a2]

    def coords(c):
        return [here[a] for a in order[c]]

    def ici(c, stage, n, ref, axis, k):
        return pltpu.make_async_remote_copy(
            src_ref=ref, dst_ref=ref, send_sem=ici_s.at[c, stage], recv_sem=ici_r.at[c, n],
            device_id=at_axis(axis, k), device_id_type=MESH)

    def sibling(c, n, ref):
        return pltpu.make_async_remote_copy(
            src_ref=ref, dst_ref=ref, send_sem=sib_s.at[c], recv_sem=sib_r.at[c, n],
            device_id=sib, device_id_type=MESH)

    def first(c, n):
        return ici(c, 0, n, box(c, *coords(c)), order[c][0], (1, 3, 2)[n])

    def second(c, n):
        a1, a2, a3 = coords(c)
        axis = order[c][1]
        if n == 0:
            return ici(c, 1, 4, box(c, everything, a2, a3), axis, 1)
        if n == 1:
            return ici(c, 1, 5, box(c, everything, a2, a3), axis, 3)
        if n == 2:
            return ici(c, 1, 6, box(c, pl.ds(0, 2), (a2 + 3) % 4, a3), axis, 1)
        return ici(c, 1, 7, box(c, pl.ds(2, 2), (a2 + 1) % 4, a3), axis, 3)

    def third(c, n, i):
        a1, a2, a3 = coords(c)
        axis = order[c][2]
        b2 = (a2 + off(i)) % 4
        if n == 0:
            return ici(c, 2, 8 + i, box(c, everything, b2, a3), axis, 1)
        if n == 1:
            return ici(c, 2, 12 + i, box(c, everything, b2, a3), axis, 3)
        if n == 2:
            return ici(c, 2, 16 + i, box(c, pl.ds(0, 2), b2, (a3 + 3) % 4), axis, 1)
        return ici(c, 2, 20 + i, box(c, pl.ds(2, 2), b2, (a3 + 1) % 4), axis, 3)

    def across(c, i, k):
        a1, a2, a3 = coords(c)
        return sibling(c, 4 * k + i, box(c, everything, (a2 + off(i)) % 4, (a3 + k) % 4))

    colors = (1, 2, 0)
    for c in colors:
        place(c)
        for n in range(3):
            first(c, n).start()
    finish = spread(tz, "z", z, 4, 1, sums_x())

    small[2].wait()
    digits = targets[...]
    table = jnp.concatenate(
        [(digits & 255), (digits >> 8) & 255, digits >> 16], axis=1).astype(f32).astype(bf16)
    first_entry = ((g * 4 + x) * 16 + v) * NV

    def find_targets(q, _):
        tok = tok_col[q].astype(jnp.int32)
        hot = jnp.where(
            (tok >> 7) == lax.broadcasted_iota(jnp.int32, (Q, 64), 1), 1.0, 0.0).astype(bf16)
        found = jnp.dot(hot, table, preferred_element_type=f32)
        mixed = found[:, :128] + 256.0 * found[:, 128:256] + 65536.0 * found[:, 256:]
        ids = jnp.sum(jnp.where(lane == (tok & 127), mixed, 0.0), axis=1, keepdims=True)
        tgt_col[q] = ids
        return 0

    lax.fori_loop(0, 4, find_targets, 0)
    acc_t[...] = jnp.zeros_like(acc_t)
    acc_s[...] = jnp.zeros_like(acc_s)

    for c in colors:
        for n in range(3):
            first(c, n).wait_recv()
        second(c, 0).start()
        second(c, 1).start()
    for c in colors:
        third(c, 0, 0).start()
        third(c, 1, 0).start()
        across(c, 0, 0).start()
    finish = spread(ty, "y", y, 4, 2, add_up(finish()))
    for c in colors:
        second(c, 0).wait_recv()
        second(c, 2).start()
        second(c, 1).wait_recv()
        second(c, 3).start()
    for c in colors:
        for i in (1, 2):
            third(c, 0, i).start()
            third(c, 1, i).start()
            across(c, i, 0).start()
    finish = spread(tgp, "g", g, 2, 3, add_up(finish()))
    for c in loads[2:]:
        c.wait()
    for c in colors:
        second(c, 2).wait_recv()
        second(c, 3).wait_recv()
        third(c, 0, 3).start()
        third(c, 1, 3).start()
        across(c, 3, 0).start()
    finish = spread(txx, "x", x, 4, 4, add_up(finish()))

    def add(acc, xs, w, rows_of):
        xs = jnp.concatenate(xs, axis=1)

        ws_ = jnp.concatenate([w[r, :] for r in rows_of], axis=0)
        acc[...] = acc[...] + jnp.dot(xs, ws_, preferred_element_type=f32)

    def chunk(gg, yy, zz):
        return gg * 16 + yy * 4 + zz

    def rows_t(n, odd):
        return pl.ds(pl.multiple_of(n * 256 + 128 * odd, 128), 128)

    def multiply(i, ks):
        y_i = (y + off(i)) % 4
        z_i = (z + off(i)) % 4
        x_i = (x + off(i)) % 4
        both = (0, 1)
        at = [(gg, y_i, (z + k) % 4) for k in ks for gg in both]
        add(acc_t, [xa[gg, yy, zz, :, 0:128].reshape(ROWS, 128) for gg, yy, zz in at],
            wt, [rows_t(chunk(*a), 0) for a in at])
        for k in ks:
            xx = (x + k) % 4
            at = [(gg, yy, z_i) for gg in both for yy in range(4)]
            add(acc_t.at[pl.ds(pl.multiple_of(xx * Q, Q), Q)],
                [xb[gg, yy, zz, xx] for gg, yy, zz in at],
                wt, [rows_t(chunk(*a), 1) for a in at])
        at = [(gg, (y + k) % 4, zz) for k in ks for gg in both for zz in range(4)]
        add(acc_s.at[pl.ds(pl.multiple_of(x_i * Q, Q), Q)],
            [xc[gg, yy, zz, x_i, 0:128] for gg, yy, zz in at],
            ws, [pl.ds(pl.multiple_of(chunk(*a) * 160, 32), 128) for a in at])

    def multiply_rest(i):
        y_i = (y + off(i)) % 4
        x_i = (x + off(i)) % 4
        at = [(gg, y_i, zz) for gg in (0, 1) for zz in range(4)]
        xs = []
        for xx in range(4):
            t = jnp.concatenate([xa[gg, yy, zz, xx, 128:144] for gg, yy, zz in at], axis=0)
            xs.append(jnp.transpose(t.astype(f32)).astype(bf16))
        add(acc_s, [jnp.concatenate(xs, axis=0)], ws,
            [pl.ds(pl.multiple_of(chunk(*a) * 160 + 128, 16), 16) for a in at])
        xs = []
        rows_of = []
        for gg in (0, 1):
            for yp in (0, 2):
                at = [(gg, yy, zz) for yy in (yp, yp + 1) for zz in range(4)]
                t = jnp.concatenate([xc[gg, yy, zz, x_i, 128:144] for gg, yy, zz in at], axis=0)
                xs.append(jnp.transpose(t.astype(f32)).astype(bf16))
                rows_of += [pl.ds(pl.multiple_of(chunk(*a) * 160 + 144, 16), 16) for a in at]
        add(acc_s.at[pl.ds(pl.multiple_of(x_i * Q, Q), Q)], xs, ws, rows_of)

    def step(i, _):
        def opposite(j):
            for c in colors:
                third(c, 2, j).wait_recv()
                third(c, 3, j).wait_recv()
                across(c, j, 2).start()

        @pl.when(i < 4)
        def _():
            for c in colors:
                across(c, i, 0).wait_recv()
            multiply(i, (0,))
            for c in colors:
                third(c, 0, i).wait_recv()
                third(c, 2, i).start()
                third(c, 1, i).wait_recv()
                third(c, 3, i).start()
                across(c, i, 3).start()
                across(c, i, 1).start()

        @pl.when((i > 0) & (i < 4))
        def _():
            opposite(i - 1)

        @pl.when((i > 0) & (i < 5))
        def _():
            for c in colors:
                for k in (1, 3):
                    across(c, i - 1, k).wait_recv()
            multiply(i - 1, (1, 3))

        @pl.when(i > 1)
        def _():
            for c in colors:
                across(c, i - 2, 2).wait_recv()
            multiply(i - 2, (2,))
            multiply_rest(i - 2)

        @pl.when(i == 4)
        def _():
            opposite(3)

        return 0

    lax.fori_loop(0, 6, step, 0)

    parts = finish()
    width = jnp.where(lax.broadcasted_iota(jnp.int32, (8, 128), 0) % 2 == 0, float(DT), float(DS))
    scale = lax.rsqrt(jnp.concatenate([p[0:2] for p in parts], axis=0) / width + EPS)
    scale = jnp.transpose(jnp.concatenate([scale, jnp.zeros((120, 128), f32)], axis=0))
    for q in range(4):
        sc_t[q] = scale[:, 2 * q : 2 * q + 1]
        sc_s[q] = scale[:, 2 * q + 1 : 2 * q + 2]

    def stats(q, m):
        r = pl.ds(pl.multiple_of(q * Q, Q), Q)
        lt = acc_t[r, :] * sc_t[q]
        ls = acc_s[r, :] * sc_s[q]
        mt = jnp.max(lt, axis=1, keepdims=True)
        ms = jnp.max(ls, axis=1, keepdims=True)
        et = jnp.exp(lt - mt)
        zt = jnp.sum(et, axis=1, keepdims=True)
        dd = jnp.sum(et * (lt - ls), axis=1, keepdims=True)
        zs = jnp.sum(jnp.exp(ls - ms), axis=1, keepdims=True)
        col = tgt_col[q].astype(jnp.int32) - first_entry
        hit = col == lax.broadcasted_iota(jnp.int32, (Q, NV), 1)
        tl = jnp.sum(jnp.where(hit, ls, 0.0), axis=1, keepdims=True)
        for n, val in enumerate((mt + jnp.log(zt), ms + jnp.log(zs), dd / zt, tl)):
            m = jnp.where(lane == 4 * n + q, val, m)
        return m

    m = lax.fori_loop(0, 4, stats, jnp.zeros((Q, 128), f32))
    val = jnp.transpose(m)[:16]

    for axis, buf, at, number, rnd in (("gx", fx, 4 * g + x, 8, 5), ("yz", fy, v, 16, 6)):
        parts = spread(buf, axis, at, number, rnd, val)()

        def lse(lo):
            top = parts[0][lo : lo + 4]
            for p in parts[1:]:
                top = jnp.maximum(top, p[lo : lo + 4])
            es = [jnp.exp(p[lo : lo + 4] - top) for p in parts]
            tot = es[0]
            for e in es[1:]:
                tot = tot + e
            return top + jnp.log(tot), es, tot

        lse_t, es, tot = lse(0)
        lse_s, _, _ = lse(4)
        cross = es[0] * parts[0][8:12]
        tl = parts[0][12:16]
        for e, p in zip(es[1:], parts[1:]):
            cross = cross + e * p[8:12]
            tl = tl + p[12:16]
        val = jnp.concatenate([lse_t, lse_s, cross / tot, tl], axis=0)

    out[...] = val

    def left(ref, sem):
        pltpu.make_async_copy(ref, ref, sem).wait()

    left(tx.at[0:3], rnd_s.at[0])
    for ref, sem in ends:
        left(ref, sem)
    for c, ref in enumerate((xa, xb, xc)):
        left(pays[c][0].at[0:3], p1_s.at[c])
        left(ref.at[0, 0, 0, 0:3], ici_s.at[c, 0])
        left(ref.at[0, 0, 0:3], ici_s.at[c, 1])
        left(ref.at[0, 0:3], ici_s.at[c, 2])
        left(ref.at[0], sib_s.at[c])


def outputs(val_ref, counts, mask_time, out_kl, out_nll, out_loss):
    x = lax.axis_index("tok")
    lane256 = lax.broadcasted_iota(jnp.int32, (1, 256), 1)
    starts = []
    total = jnp.int32(0)
    for t in range(4):
        starts.append(total)
        total = total + counts[t]
    val = val_ref[...]
    lse_t, lse_s, cross, tl = (val[4 * n : 4 * n + 4] for n in range(4))
    kl = cross - lse_t + lse_s
    nll = lse_s - tl
    kl_total = jnp.sum(jnp.sum(kl, axis=1, keepdims=True), axis=0, keepdims=True)
    nll_total = jnp.sum(jnp.sum(nll, axis=1, keepdims=True), axis=0, keepdims=True)
    time = jnp.full((1, 1), mask_time[0], jnp.int32).astype(f32)
    masked = jnp.full((1, 1), total, jnp.int32).astype(f32)
    weight = 1000.0 / time
    out_loss[...] = jnp.concatenate([weight * nll_total / 8192.0, kl_total / masked], axis=1)

    cols = jnp.transpose(jnp.concatenate([kl, nll, jnp.zeros((120, 128), f32)], axis=0))
    start = jnp.int32(0)
    count = jnp.int32(0)
    for t in range(4):
        start = start + jnp.where(x == t, starts[t], 0)
        count = count + jnp.where(x == t, counts[t], 0)
    slot = lax.broadcasted_iota(jnp.int32, (Q, 256), 1)
    gap = lax.broadcasted_iota(jnp.int32, (Q, 256), 0) - slot
    for n, out in ((0, out_kl), (4, out_nll)):
        s = jnp.zeros((Q, 256), f32)
        for q in range(4):
            s = s + jnp.where(gap == start - q * Q, cols[:, n + q : n + q + 1], 0.0)
        s = jnp.sum(s, axis=0, keepdims=True)
        out[...] = jnp.where(lane256 < count, s, 0.0)


def shards(th, sh, tg, sg, wt, ws, targets, positions, counts, mask_time):
    vm = pl.BlockSpec(memory_space=pltpu.VMEM)
    sm = pl.BlockSpec(memory_space=pltpu.SMEM)
    anyspace = pl.BlockSpec(memory_space=pl.ANY)
    dma = pltpu.SemaphoreType.DMA
    val = pl.pallas_call(
        body,
        out_shape=jax.ShapeDtypeStruct((16, 128), f32),
        in_specs=[anyspace, anyspace, anyspace, vm, anyspace, anyspace, anyspace, anyspace, sm],
        out_specs=vm,
        scratch_shapes=[
            pltpu.VMEM((2048, 256), bf16),
            pltpu.VMEM((160, 2048), bf16),
            pltpu.VMEM((2, 128), bf16),
            pltpu.VMEM((64, 128), jnp.int32),
            pltpu.VMEM((8, 128), jnp.int32),
            pltpu.VMEM((ROWS, 2048), bf16),
            pltpu.VMEM((DT, NV), bf16),
            pltpu.VMEM((DS, NV), bf16),
            pltpu.VMEM((2, 4, 4, 4, XT, 128), bf16),
            pltpu.VMEM((2, 4, 4, 4, 128, 128), bf16),
            pltpu.VMEM((2, 4, 4, 4, XT, 128), bf16),
            pltpu.VMEM((ROWS, NV), f32),
            pltpu.VMEM((ROWS, NV), f32),
            pltpu.VMEM((4, Q, 1), f32),
            pltpu.VMEM((4, Q, 1), f32),
            pltpu.VMEM((4, Q, 1), f32),
            pltpu.VMEM((4, Q, 1), f32),
            pltpu.VMEM((4, 128, 128), bf16),
            pltpu.VMEM((4, 128, 128), bf16),
            pltpu.VMEM((4, 160, 128), bf16),
            pltpu.VMEM((4, 128, 128), bf16),
            pltpu.VMEM((4, 128, 128), bf16),
            pltpu.VMEM((4, 160, 128), bf16),
            pltpu.VMEM((8, 8, 128), f32),
            pltpu.VMEM((4, 8, 128), f32),
            pltpu.VMEM((4, 8, 128), f32),
            pltpu.VMEM((2, 8, 128), f32),
            pltpu.VMEM((4, 8, 128), f32),
            pltpu.VMEM((8, 16, 128), f32),
            pltpu.VMEM((16, 16, 128), f32),
            dma((13,)),
            dma((3,)),
            dma((3, 3)),
            dma((7,)),
            dma((35,)),
            dma((3, 3)),
            dma((3, N_ICI)),
            dma((3,)),
            dma((3, N_SIB)),
        ],
        compiler_params=pltpu.CompilerParams(
            collective_id=0, has_side_effects=True, vmem_limit_bytes=58 * 1024 * 1024),
        name="elbo",
    )(
        th, sh.T, tg.reshape(2, 128), sg, wt, ws,
        targets.reshape(64, 128), positions.reshape(8, 128), counts,
    )
    kl, nll, loss = pl.pallas_call(
        outputs,
        out_shape=(
            jax.ShapeDtypeStruct((1, 256), f32),
            jax.ShapeDtypeStruct((1, 256), f32),
            jax.ShapeDtypeStruct((1, 2), f32),
        ),
        in_specs=[vm, sm, sm],
        out_specs=(vm, vm, vm),
        name="slots",
    )(val, counts, mask_time)
    return kl.reshape(256), nll.reshape(256), loss.reshape(2)


def solution(mesh):
    feats = ("group", "vocab")
    cols = ("group", "tok", "vocab")
    in_specs = (
        P("tok", feats), P("tok", feats), P(feats), P(feats),
        P(None, cols), P(None, cols), P(), P(), P(), P(),
    )
    out_specs = (P("tok"), P("tok"), P())
    return jax.shard_map(shards, mesh=mesh, in_specs=in_specs, out_specs=out_specs, check_vma=False)
```

```python
import functools

import jax
import jax.numpy as jnp
from jax import lax
from jax.experimental import pallas as pl
from jax.experimental.pallas import tpu as pltpu
from jax.sharding import PartitionSpec as P

EPS = 1e-06
MESH = pl.DeviceIdType.MESH
f32 = jnp.float32
bf16 = jnp.bfloat16

ROWS = 512
PLANE = (10, 6, 14, 9, 11, 2, 8, 5, 7, 13, 15, 1, 3, 4, 12)
Q = 128
DT = 8192
DS = 5120
NV = 768
NT = 256
XT = 144

N_ICI = 24
N_SIB = 16


def off(i):
    return jnp.where(i < 2, i, 5 - i)


def body(
    th, sh, tg_any, sg, wt_hbm, ws_hbm, targets_any, positions_any, counts,
    out,
    ht, hs, tg, targets, positions, hot, wt, ws, xa, xb, xc, acc_t, acc_s, tok_col, tgt_col,
    sc_t, sc_s, pay_a, pay_b, pay_c, p1a, p1b, p1c, tx, tz, ty, tgp, txx, fx, fy,
    load_sem, p1_s, p1_r, rnd_s, rnd_r, ici_s, ici_r, sib_s, sib_r,
):
    g = lax.axis_index("group")
    x = lax.axis_index("tok")
    v = lax.axis_index("vocab")
    y = v // 4
    z = v % 4
    sib = {"group": 1 - g}

    def at_axis(axis, k):
        if axis == "x":
            return {"tok": (x + k) % 4}
        if axis == "y":
            return {"vocab": ((y + k) % 4) * 4 + z}
        return {"vocab": y * 4 + (z + k) % 4}

    def at_plane(k):
        return {"vocab": ((y + k // 4) % 4) * 4 + (z + k % 4) % 4}

    barrier = pltpu.get_barrier_semaphore()
    peers = [at_axis("x", k) for k in (1, 2, 3)] + [at_plane(k) for k in range(1, 16)] + [sib]
    peers += [{"group": 1 - g, "tok": (x + k) % 4} for k in (1, 2, 3)]
    for d in peers:
        pl.semaphore_signal(barrier, inc=1, device_id=d, device_id_type=MESH)

    small = [
        pltpu.make_async_copy(positions_any, positions, load_sem.at[10]),
        pltpu.make_async_copy(tg_any, tg, load_sem.at[11]),
        pltpu.make_async_copy(targets_any, targets, load_sem.at[12]),
    ]
    loads = [
        pltpu.make_async_copy(th, ht, load_sem.at[0]),
        pltpu.make_async_copy(sh, hs, load_sem.at[1]),
    ]
    for i in range(4):
        r = pl.ds(i * (DT // 4), DT // 4)
        loads.append(pltpu.make_async_copy(wt_hbm.at[r], wt.at[r], load_sem.at[2 + i]))
        r = pl.ds(i * (DS // 4), DS // 4)
        loads.append(pltpu.make_async_copy(ws_hbm.at[r], ws.at[r], load_sem.at[6 + i]))
    for c in small + loads:
        c.start()

    starts = []
    total = jnp.int32(0)
    for t in range(4):
        starts.append(total)
        total = total + counts[t]
    lane256 = lax.broadcasted_iota(jnp.int32, (1, 256), 1)
    small[0].wait()
    pos_rows = []
    for t in range(4):
        p = jnp.concatenate([positions[2 * t : 2 * t + 1, :], positions[2 * t + 1 : 2 * t + 2, :]], axis=1)
        pos_rows.append(jnp.where(lane256 < counts[t], p + 2048 * t, 0))

    def tokens(q, _):
        d = (
            lax.broadcasted_iota(jnp.int32, (Q, 256), 0)
            + q * Q
            - lax.broadcasted_iota(jnp.int32, (Q, 256), 1)
        )
        s = jnp.zeros((Q, 256), jnp.int32)
        for t in range(4):
            s = s + jnp.where(d == starts[t], pos_rows[t], 0)
        tok_col[q] = jnp.sum(s.astype(f32), axis=1, keepdims=True)
        return 0

    lax.fori_loop(0, 4, tokens, 0)

    lane = lax.broadcasted_iota(jnp.int32, (Q, 128), 1)

    def tiny_copy(q, k):
        return pltpu.make_async_remote_copy(
            src_ref=tx.at[4 + q], dst_ref=tx.at[x], send_sem=rnd_s.at[0], recv_sem=rnd_r.at[k],
            device_id={"tok": q}, device_id_type=MESH)

    pays = ((pay_a, p1a), (pay_b, p1b), (pay_c, p1c))

    def pay_copy(c, q, k):
        src, dst = pays[c]
        return pltpu.make_async_remote_copy(
            src_ref=src.at[q], dst_ref=dst.at[x], send_sem=p1_s.at[c], recv_sem=p1_r.at[c, k],
            device_id={"tok": q}, device_id_type=MESH)

    def to(k):
        return (x + (2, 1, 3)[k]) % 4

    def make_hot(q, _):
        tok = tok_col[q].astype(jnp.int32) - 2048 * x
        hot[pl.ds(pl.multiple_of(q * Q, Q), Q), :] = jnp.where(
            tok == lax.broadcasted_iota(jnp.int32, (Q, 2048), 1), 1.0, 0.0).astype(bf16)
        return 0

    lax.fori_loop(0, 4, make_hot, 0)
    loads[0].wait()
    ct = jnp.dot(hot[...], ht[...], preferred_element_type=f32)
    for q in range(4):
        cq = ct[q * Q : (q + 1) * Q]
        sc_t[q] = jnp.sum(cq * cq, axis=1, keepdims=True)
        pay_a[q] = cq[:, :128].astype(bf16)
        pay_b[q] = cq[:, 128:].astype(bf16)
    pl.semaphore_wait(barrier, len(peers))
    for k in range(3):
        pay_copy(1, to(k), k).start()
    loads[1].wait()
    cs = lax.dot_general(hot[...], hs[...], (((1,), (1,)), ((), ())), preferred_element_type=f32)
    for q in range(4):
        cq = cs[q * Q : (q + 1) * Q]
        sq_s = jnp.sum(cq * cq, axis=1, keepdims=True)
        rest = jnp.concatenate([cq[:, 128:160], jnp.zeros((Q, 96), f32)], axis=1)
        rest = jnp.where(lane == 32, sc_t[q], jnp.where(lane == 33, sq_s, rest))
        rest = jnp.transpose(rest)
        tx[4 + q] = rest[32:40]
        pay_c[q, 0:128] = cq[:, :128].astype(bf16)
        pay_c[q, 128:160] = rest[:32].astype(bf16)
    for k in range(3):
        pay_copy(2, to(k), k).start()
    for k in range(3):
        tiny_copy(to(k), k).start()
    for k in range(3):
        pay_copy(0, to(k), k).start()

    ends = []

    used = [3]

    def spread(buf, axis, at, number, rnd, value):
        buf[at] = value
        if axis == "g":
            devs = [sib]
        elif axis == "gx":
            devs = [{"group": 1 - g, "tok": (x + k) % 4} for k in (2, 1, 3)]
            devs += [at_axis("x", k) for k in (2, 1, 3)] + [sib]
        elif axis == "yz":
            devs = [at_plane(k) for k in PLANE]
        else:
            devs = [at_axis(axis, k) for k in (2, 1, 3)]
        cps = [pltpu.make_async_remote_copy(
            src_ref=buf.at[at], dst_ref=buf.at[at], send_sem=rnd_s.at[rnd], recv_sem=rnd_r.at[used[0] + n],
            device_id=d, device_id_type=MESH) for n, d in enumerate(devs)]
        used[0] += len(devs)
        for c in cps:
            c.start()
        ends.append((buf.at[0 : len(devs)], rnd_s.at[rnd]))

        def finish():
            for c in cps:
                c.wait_recv()
            return [buf[i] for i in range(number)]

        return finish

    def add_up(parts):
        total = parts[0]
        for p in parts[1:]:
            total = total + p
        return total

    def sums_x():
        for k in range(3):
            tiny_copy((x + 1) % 4, k).wait_recv()
        return add_up([tx[4 + x]] + [tx[(x + k) % 4] for k in (1, 2, 3)])

    small[1].wait()
    gain_t = tg[...].astype(f32)
    gain_s = sg[...].astype(f32).reshape(1, 160)
    eye = lax.broadcasted_iota(jnp.int32, (32, 32), 0) == lax.broadcasted_iota(jnp.int32, (32, 32), 1)
    gain_col = jnp.sum(jnp.where(eye, gain_s[:, 128:160], 0.0), axis=1, keepdims=True)

    def mine(c, lo, hi):
        own, others = pays[c]
        s = own[x, lo:hi].astype(f32)
        for k in (1, 2, 3):
            s = s + others[(x + k) % 4, lo:hi].astype(f32)
        return s

    def place(c):
        for k in range(3):
            pay_copy(c, to(k), k).wait_recv()
        if c == 0:
            xa[g, y, z, x, 0:128] = (mine(0, 0, 128) * gain_t[0:1]).astype(bf16)
        elif c == 1:
            xb[g, y, z, x] = (mine(1, 0, 128) * gain_t[1:2]).astype(bf16)
        else:
            xc[g, y, z, x, 0:128] = (mine(2, 0, 128) * gain_s[:, :128]).astype(bf16)
            rest = (mine(2, 128, 160) * gain_col).astype(bf16)
            xa[g, y, z, x, 128:144] = rest[:16]
            xc[g, y, z, x, 128:144] = rest[16:]

    order = ("xyz", "yzx", "zxy")
    here = {"x": x, "y": y, "z": z}
    everything = slice(None)

    def box(c, a1, a2, a3):
        if c == 0:
            return xa.at[g, a2, a3, a1]
        if c == 1:
            return xb.at[g, a1, a2, a3]
        return xc.at[g, a3, a1, a2]

    def coords(c):
        return [here[a] for a in order[c]]

    def ici(c, stage, n, ref, axis, k):
        return pltpu.make_async_remote_copy(
            src_ref=ref, dst_ref=ref, send_sem=ici_s.at[c, stage], recv_sem=ici_r.at[c, n],
            device_id=at_axis(axis, k), device_id_type=MESH)

    def sibling(c, n, ref):
        return pltpu.make_async_remote_copy(
            src_ref=ref, dst_ref=ref, send_sem=sib_s.at[c], recv_sem=sib_r.at[c, n],
            device_id=sib, device_id_type=MESH)

    def first(c, n):
        return ici(c, 0, n, box(c, *coords(c)), order[c][0], (2, 1, 3)[n])

    def second(c, n):
        a1, a2, a3 = coords(c)
        axis = order[c][1]
        if n == 0:
            return ici(c, 1, 4, box(c, everything, a2, a3), axis, 1)
        if n == 1:
            return ici(c, 1, 5, box(c, everything, a2, a3), axis, 3)
        if n == 2:
            return ici(c, 1, 6, box(c, pl.ds(0, 2), (a2 + 3) % 4, a3), axis, 1)
        return ici(c, 1, 7, box(c, pl.ds(2, 2), (a2 + 1) % 4, a3), axis, 3)

    def third(c, n, i):
        a1, a2, a3 = coords(c)
        axis = order[c][2]
        b2 = (a2 + off(i)) % 4
        if n == 0:
            return ici(c, 2, 8 + i, box(c, everything, b2, a3), axis, 1)
        if n == 1:
            return ici(c, 2, 12 + i, box(c, everything, b2, a3), axis, 3)
        if n == 2:
            return ici(c, 2, 16 + i, box(c, pl.ds(0, 2), b2, (a3 + 3) % 4), axis, 1)
        return ici(c, 2, 20 + i, box(c, pl.ds(2, 2), b2, (a3 + 1) % 4), axis, 3)

    def across(c, i, k):
        a1, a2, a3 = coords(c)
        return sibling(c, 4 * k + i, box(c, everything, (a2 + off(i)) % 4, (a3 + k) % 4))

    colors = (1, 2, 0)
    for c in colors:
        place(c)
        for n in range(3):
            first(c, n).start()
    finish = spread(tz, "z", z, 4, 1, sums_x())

    small[2].wait()
    digits = targets[...]
    table = jnp.concatenate(
        [(digits & 255), (digits >> 8) & 255, digits >> 16], axis=1).astype(f32).astype(bf16)
    first_entry = ((g * 4 + x) * 16 + v) * NV

    def find_targets(q, _):
        tok = tok_col[q].astype(jnp.int32)
        hot = jnp.where(
            (tok >> 7) == lax.broadcasted_iota(jnp.int32, (Q, 64), 1), 1.0, 0.0).astype(bf16)
        found = jnp.dot(hot, table, preferred_element_type=f32)
        mixed = found[:, :128] + 256.0 * found[:, 128:256] + 65536.0 * found[:, 256:]
        ids = jnp.sum(jnp.where(lane == (tok & 127), mixed, 0.0), axis=1, keepdims=True)
        tgt_col[q] = ids
        return 0

    lax.fori_loop(0, 4, find_targets, 0)
    acc_t[...] = jnp.zeros_like(acc_t)
    acc_s[...] = jnp.zeros_like(acc_s)

    for c in colors:
        for n in range(3):
            first(c, n).wait_recv()
        second(c, 0).start()
        second(c, 1).start()
    for c in colors:
        third(c, 0, 0).start()
        third(c, 1, 0).start()
        across(c, 0, 0).start()
    finish = spread(ty, "y", y, 4, 2, add_up(finish()))
    def near():
        for c in colors:
            second(c, 0).wait_recv()
            second(c, 2).start()
            second(c, 1).wait_recv()
            second(c, 3).start()
        for c in colors:
            for i in (1, 2):
                third(c, 0, i).start()
                third(c, 1, i).start()
                across(c, i, 0).start()

    def far():
        for c in colors:
            second(c, 2).wait_recv()
            second(c, 3).wait_recv()
            third(c, 0, 3).start()
            third(c, 1, 3).start()
            across(c, 3, 0).start()

    for c in loads[2:]:
        c.wait()

    def add(acc, xs, w, rows_of):
        xs = jnp.concatenate(xs, axis=1)

        ws_ = jnp.concatenate([w[r, :] for r in rows_of], axis=0)
        acc[...] = acc[...] + jnp.dot(xs, ws_, preferred_element_type=f32)

    def chunk(gg, yy, zz):
        return gg * 16 + yy * 4 + zz

    def rows_t(n, odd):
        return pl.ds(pl.multiple_of(n * 256 + 128 * odd, 128), 128)

    def multiply(i, ks):
        y_i = (y + off(i)) % 4
        z_i = (z + off(i)) % 4
        x_i = (x + off(i)) % 4
        both = (0, 1)
        at = [(gg, y_i, (z + k) % 4) for k in ks for gg in both]
        add(acc_t, [xa[gg, yy, zz, :, 0:128].reshape(ROWS, 128) for gg, yy, zz in at],
            wt, [rows_t(chunk(*a), 0) for a in at])
        for k in ks:
            xx = (x + k) % 4
            at = [(gg, yy, z_i) for gg in both for yy in range(4)]
            add(acc_t.at[pl.ds(pl.multiple_of(xx * Q, Q), Q)],
                [xb[gg, yy, zz, xx] for gg, yy, zz in at],
                wt, [rows_t(chunk(*a), 1) for a in at])
        at = [(gg, (y + k) % 4, zz) for k in ks for gg in both for zz in range(4)]
        add(acc_s.at[pl.ds(pl.multiple_of(x_i * Q, Q), Q)],
            [xc[gg, yy, zz, x_i, 0:128] for gg, yy, zz in at],
            ws, [pl.ds(pl.multiple_of(chunk(*a) * 160, 32), 128) for a in at])

    def multiply_rest(i):
        y_i = (y + off(i)) % 4
        x_i = (x + off(i)) % 4
        at = [(gg, y_i, zz) for gg in (0, 1) for zz in range(4)]
        xs = []
        for xx in range(4):
            t = jnp.concatenate([xa[gg, yy, zz, xx, 128:144] for gg, yy, zz in at], axis=0)
            xs.append(jnp.transpose(t.astype(f32)).astype(bf16))
        add(acc_s, [jnp.concatenate(xs, axis=0)], ws,
            [pl.ds(pl.multiple_of(chunk(*a) * 160 + 128, 16), 16) for a in at])
        xs = []
        rows_of = []
        for gg in (0, 1):
            for yp in (0, 2):
                at = [(gg, yy, zz) for yy in (yp, yp + 1) for zz in range(4)]
                t = jnp.concatenate([xc[gg, yy, zz, x_i, 128:144] for gg, yy, zz in at], axis=0)
                xs.append(jnp.transpose(t.astype(f32)).astype(bf16))
                rows_of += [pl.ds(pl.multiple_of(chunk(*a) * 160 + 144, 16), 16) for a in at]
        add(acc_s.at[pl.ds(pl.multiple_of(x_i * Q, Q), Q)], xs, ws, rows_of)

    def step(e, _):
        @pl.when(e < 4)
        def _():
            for c in colors:
                across(c, e, 0).wait_recv()
            multiply(e, (0,))

        @pl.when(e == 0)
        def _():
            near()

        @pl.when((e > 0) & (e < 5))
        def _():
            i = e - 1
            for c in colors:
                third(c, 0, i).wait_recv()
                third(c, 2, i).start()
                third(c, 1, i).wait_recv()
                third(c, 3, i).start()
            for c in colors:
                across(c, i, 3).start()
                across(c, i, 1).start()

        @pl.when(e == 1)
        def _():
            far()

        @pl.when((e > 1) & (e < 6))
        def _():
            i = e - 2
            for c in colors:
                for k in (1, 3):
                    across(c, i, k).wait_recv()
            multiply(i, (1, 3))

        @pl.when((e > 2) & (e < 7))
        def _():
            i = e - 3
            for c in colors:
                third(c, 2, i).wait_recv()
                third(c, 3, i).wait_recv()
                across(c, i, 2).start()

        @pl.when(e > 3)
        def _():
            i = e - 4
            for c in colors:
                across(c, i, 2).wait_recv()
            multiply(i, (2,))
            multiply_rest(i)

        return 0

    lax.fori_loop(0, 2, step, 0)
    finish = spread(tgp, "g", g, 2, 3, add_up(finish()))
    finish = spread(txx, "x", x, 4, 4, add_up(finish()))
    lax.fori_loop(2, 8, step, 0)

    parts = finish()
    width = jnp.where(lax.broadcasted_iota(jnp.int32, (8, 128), 0) % 2 == 0, float(DT), float(DS))
    scale = lax.rsqrt(jnp.concatenate([p[0:2] for p in parts], axis=0) / width + EPS)
    scale = jnp.transpose(jnp.concatenate([scale, jnp.zeros((120, 128), f32)], axis=0))
    for q in range(4):
        sc_t[q] = scale[:, 2 * q : 2 * q + 1]
        sc_s[q] = scale[:, 2 * q + 1 : 2 * q + 2]

    def stats(q, m):
        r = pl.ds(pl.multiple_of(q * Q, Q), Q)
        lt = acc_t[r, :] * sc_t[q]
        ls = acc_s[r, :] * sc_s[q]
        mt = jnp.max(lt, axis=1, keepdims=True)
        ms = jnp.max(ls, axis=1, keepdims=True)
        et = jnp.exp(lt - mt)
        zt = jnp.sum(et, axis=1, keepdims=True)
        dd = jnp.sum(et * (lt - ls), axis=1, keepdims=True)
        zs = jnp.sum(jnp.exp(ls - ms), axis=1, keepdims=True)
        col = tgt_col[q].astype(jnp.int32) - first_entry
        hit = col == lax.broadcasted_iota(jnp.int32, (Q, NV), 1)
        tl = jnp.sum(jnp.where(hit, ls, 0.0), axis=1, keepdims=True)
        for n, val in enumerate((mt + jnp.log(zt), ms + jnp.log(zs), dd / zt, tl)):
            m = jnp.where(lane == 4 * n + q, val, m)
        return m

    m = lax.fori_loop(0, 4, stats, jnp.zeros((Q, 128), f32))
    val = jnp.transpose(m)[:16]

    for axis, buf, at, number, rnd in (("gx", fx, 4 * g + x, 8, 5), ("yz", fy, v, 16, 6)):
        parts = spread(buf, axis, at, number, rnd, val)()

        def lse(lo):
            top = parts[0][lo : lo + 4]
            for p in parts[1:]:
                top = jnp.maximum(top, p[lo : lo + 4])
            es = [jnp.exp(p[lo : lo + 4] - top) for p in parts]
            tot = es[0]
            for e in es[1:]:
                tot = tot + e
            return top + jnp.log(tot), es, tot

        lse_t, es, tot = lse(0)
        lse_s, _, _ = lse(4)
        cross = es[0] * parts[0][8:12]
        tl = parts[0][12:16]
        for e, p in zip(es[1:], parts[1:]):
            cross = cross + e * p[8:12]
            tl = tl + p[12:16]
        val = jnp.concatenate([lse_t, lse_s, cross / tot, tl], axis=0)

    out[...] = val

    def left(ref, sem):
        pltpu.make_async_copy(ref, ref, sem).wait()

    left(tx.at[0:3], rnd_s.at[0])
    for ref, sem in ends:
        left(ref, sem)
    for c, ref in enumerate((xa, xb, xc)):
        left(pays[c][0].at[0:3], p1_s.at[c])
        left(ref.at[0, 0, 0, 0:3], ici_s.at[c, 0])
        left(ref.at[0, 0, 0:3], ici_s.at[c, 1])
        left(ref.at[0, 0:3], ici_s.at[c, 2])
        left(ref.at[0], sib_s.at[c])


def outputs(val_ref, counts, mask_time, out_kl, out_nll, out_loss):
    x = lax.axis_index("tok")
    lane256 = lax.broadcasted_iota(jnp.int32, (1, 256), 1)
    starts = []
    total = jnp.int32(0)
    for t in range(4):
        starts.append(total)
        total = total + counts[t]
    val = val_ref[...]
    lse_t, lse_s, cross, tl = (val[4 * n : 4 * n + 4] for n in range(4))
    kl = cross - lse_t + lse_s
    nll = lse_s - tl
    kl_total = jnp.sum(jnp.sum(kl, axis=1, keepdims=True), axis=0, keepdims=True)
    nll_total = jnp.sum(jnp.sum(nll, axis=1, keepdims=True), axis=0, keepdims=True)
    time = jnp.full((1, 1), mask_time[0], jnp.int32).astype(f32)
    masked = jnp.full((1, 1), total, jnp.int32).astype(f32)
    weight = 1000.0 / time
    out_loss[...] = jnp.concatenate([weight * nll_total / 8192.0, kl_total / masked], axis=1)

    cols = jnp.transpose(jnp.concatenate([kl, nll, jnp.zeros((120, 128), f32)], axis=0))
    start = jnp.int32(0)
    count = jnp.int32(0)
    for t in range(4):
        start = start + jnp.where(x == t, starts[t], 0)
        count = count + jnp.where(x == t, counts[t], 0)
    slot = lax.broadcasted_iota(jnp.int32, (Q, 256), 1)
    gap = lax.broadcasted_iota(jnp.int32, (Q, 256), 0) - slot
    for n, out in ((0, out_kl), (4, out_nll)):
        s = jnp.zeros((Q, 256), f32)
        for q in range(4):
            s = s + jnp.where(gap == start - q * Q, cols[:, n + q : n + q + 1], 0.0)
        s = jnp.sum(s, axis=0, keepdims=True)
        out[...] = jnp.where(lane256 < count, s, 0.0)


def shards(th, sh, tg, sg, wt, ws, targets, positions, counts, mask_time):
    vm = pl.BlockSpec(memory_space=pltpu.VMEM)
    sm = pl.BlockSpec(memory_space=pltpu.SMEM)
    anyspace = pl.BlockSpec(memory_space=pl.ANY)
    dma = pltpu.SemaphoreType.DMA
    val = pl.pallas_call(
        body,
        out_shape=jax.ShapeDtypeStruct((16, 128), f32),
        in_specs=[anyspace, anyspace, anyspace, vm, anyspace, anyspace, anyspace, anyspace, sm],
        out_specs=vm,
        scratch_shapes=[
            pltpu.VMEM((2048, 256), bf16),
            pltpu.VMEM((160, 2048), bf16),
            pltpu.VMEM((2, 128), bf16),
            pltpu.VMEM((64, 128), jnp.int32),
            pltpu.VMEM((8, 128), jnp.int32),
            pltpu.VMEM((ROWS, 2048), bf16),
            pltpu.VMEM((DT, NV), bf16),
            pltpu.VMEM((DS, NV), bf16),
            pltpu.VMEM((2, 4, 4, 4, XT, 128), bf16),
            pltpu.VMEM((2, 4, 4, 4, 128, 128), bf16),
            pltpu.VMEM((2, 4, 4, 4, XT, 128), bf16),
            pltpu.VMEM((ROWS, NV), f32),
            pltpu.VMEM((ROWS, NV), f32),
            pltpu.VMEM((4, Q, 1), f32),
            pltpu.VMEM((4, Q, 1), f32),
            pltpu.VMEM((4, Q, 1), f32),
            pltpu.VMEM((4, Q, 1), f32),
            pltpu.VMEM((4, 128, 128), bf16),
            pltpu.VMEM((4, 128, 128), bf16),
            pltpu.VMEM((4, 160, 128), bf16),
            pltpu.VMEM((4, 128, 128), bf16),
            pltpu.VMEM((4, 128, 128), bf16),
            pltpu.VMEM((4, 160, 128), bf16),
            pltpu.VMEM((8, 8, 128), f32),
            pltpu.VMEM((4, 8, 128), f32),
            pltpu.VMEM((4, 8, 128), f32),
            pltpu.VMEM((2, 8, 128), f32),
            pltpu.VMEM((4, 8, 128), f32),
            pltpu.VMEM((8, 16, 128), f32),
            pltpu.VMEM((16, 16, 128), f32),
            dma((13,)),
            dma((3,)),
            dma((3, 3)),
            dma((7,)),
            dma((35,)),
            dma((3, 3)),
            dma((3, N_ICI)),
            dma((3,)),
            dma((3, N_SIB)),
        ],
        compiler_params=pltpu.CompilerParams(
            collective_id=0, has_side_effects=True, vmem_limit_bytes=58 * 1024 * 1024),
        name="elbo",
    )(
        th, sh.T, tg.reshape(2, 128), sg, wt, ws,
        targets.reshape(64, 128), positions.reshape(8, 128), counts,
    )
    kl, nll, loss = pl.pallas_call(
        outputs,
        out_shape=(
            jax.ShapeDtypeStruct((1, 256), f32),
            jax.ShapeDtypeStruct((1, 256), f32),
            jax.ShapeDtypeStruct((1, 2), f32),
        ),
        in_specs=[vm, sm, sm],
        out_specs=(vm, vm, vm),
        name="slots",
    )(val, counts, mask_time)
    return kl.reshape(256), nll.reshape(256), loss.reshape(2)


def solution(mesh):
    feats = ("group", "vocab")
    cols = ("group", "tok", "vocab")
    in_specs = (
        P("tok", feats), P("tok", feats), P(feats), P(feats),
        P(None, cols), P(None, cols), P(), P(), P(), P(),
    )
    out_specs = (P("tok"), P("tok"), P())
    return jax.shard_map(shards, mesh=mesh, in_specs=in_specs, out_specs=out_specs, check_vma=False)
```

```python
import functools

import jax
import jax.numpy as jnp
from jax import lax
from jax.experimental import pallas as pl
from jax.experimental.pallas import tpu as pltpu
from jax.sharding import PartitionSpec as P

EPS = 1e-06
MESH = pl.DeviceIdType.MESH
f32 = jnp.float32
bf16 = jnp.bfloat16

ROWS = 512
PLANE = (10, 6, 14, 9, 11, 2, 8, 5, 7, 13, 15, 1, 3, 4, 12)
Q = 128
DT = 8192
DS = 5120
NV = 768
NT = 256
XT = 144

N_ICI = 24
N_SIB = 16


def off(i):
    return jnp.where(i < 2, i, 5 - i)


def body(
    th, sh, tg_any, sg, wt_hbm, ws_hbm, targets_any, positions_any, counts,
    out,
    ht, hs, tg, targets, positions, hot, wt, ws, xa, xb, xc, acc_t, acc_s, tok_col, tgt_col,
    sc_t, sc_s, pay_a, pay_b, pay_c, p1a, p1b, p1c, tx, tz, ty, tgp, txx, fx, fy,
    load_sem, p1_s, p1_r, rnd_s, rnd_r, ici_s, ici_r, sib_s, sib_r,
):
    g = lax.axis_index("group")
    x = lax.axis_index("tok")
    v = lax.axis_index("vocab")
    y = v // 4
    z = v % 4
    sib = {"group": 1 - g}

    def at_axis(axis, k):
        if axis == "x":
            return {"tok": (x + k) % 4}
        if axis == "y":
            return {"vocab": ((y + k) % 4) * 4 + z}
        return {"vocab": y * 4 + (z + k) % 4}

    def at_plane(k):
        return {"vocab": ((y + k // 4) % 4) * 4 + (z + k % 4) % 4}

    barrier = pltpu.get_barrier_semaphore()
    peers = [at_axis("x", k) for k in (1, 2, 3)] + [at_plane(k) for k in range(1, 16)] + [sib]
    peers += [{"group": 1 - g, "tok": (x + k) % 4} for k in (1, 2, 3)]
    small = [
        pltpu.make_async_copy(positions_any, positions, load_sem.at[10]),
        pltpu.make_async_copy(tg_any, tg, load_sem.at[11]),
        pltpu.make_async_copy(targets_any, targets, load_sem.at[12]),
    ]
    loads = [
        pltpu.make_async_copy(th, ht, load_sem.at[0]),
        pltpu.make_async_copy(sh, hs, load_sem.at[1]),
    ]
    for i in range(4):
        r = pl.ds(i * (DT // 4), DT // 4)
        loads.append(pltpu.make_async_copy(wt_hbm.at[r], wt.at[r], load_sem.at[2 + i]))
        r = pl.ds(i * (DS // 4), DS // 4)
        loads.append(pltpu.make_async_copy(ws_hbm.at[r], ws.at[r], load_sem.at[6 + i]))
    for c in small[:1] + loads[:2] + small[1:] + loads[2:]:
        c.start()
    for d in peers:
        pl.semaphore_signal(barrier, inc=1, device_id=d, device_id_type=MESH)

    starts = []
    total = jnp.int32(0)
    for t in range(4):
        starts.append(total)
        total = total + counts[t]
    lane256 = lax.broadcasted_iota(jnp.int32, (1, 256), 1)
    small[0].wait()
    pos_rows = []
    for t in range(4):
        p = jnp.concatenate([positions[2 * t : 2 * t + 1, :], positions[2 * t + 1 : 2 * t + 2, :]], axis=1)
        pos_rows.append(jnp.where(lane256 < counts[t], p + 2048 * t, 0))

    def tokens(q, _):
        d = (
            lax.broadcasted_iota(jnp.int32, (Q, 256), 0)
            + q * Q
            - lax.broadcasted_iota(jnp.int32, (Q, 256), 1)
        )
        s = jnp.zeros((Q, 256), jnp.int32)
        for t in range(4):
            s = s + jnp.where(d == starts[t], pos_rows[t], 0)
        tok_col[q] = jnp.sum(s.astype(f32), axis=1, keepdims=True)
        return 0

    lax.fori_loop(0, 4, tokens, 0)

    lane = lax.broadcasted_iota(jnp.int32, (Q, 128), 1)

    def tiny_copy(q, k):
        return pltpu.make_async_remote_copy(
            src_ref=tx.at[4 + q], dst_ref=tx.at[x], send_sem=rnd_s.at[0], recv_sem=rnd_r.at[k],
            device_id={"tok": q}, device_id_type=MESH)

    pays = ((pay_a, p1a), (pay_b, p1b), (pay_c, p1c))

    def pay_copy(c, q, k):
        src, dst = pays[c]
        return pltpu.make_async_remote_copy(
            src_ref=src.at[q], dst_ref=dst.at[x], send_sem=p1_s.at[c], recv_sem=p1_r.at[c, k],
            device_id={"tok": q}, device_id_type=MESH)

    def to(k):
        return (x + (2, 1, 3)[k]) % 4

    def make_hot(q, _):
        tok = tok_col[q].astype(jnp.int32) - 2048 * x
        hot[pl.ds(pl.multiple_of(q * Q, Q), Q), :] = jnp.where(
            tok == lax.broadcasted_iota(jnp.int32, (Q, 2048), 1), 1.0, 0.0).astype(bf16)
        return 0

    lax.fori_loop(0, 4, make_hot, 0)
    loads[0].wait()
    ct = jnp.dot(hot[...], ht[...], preferred_element_type=f32)
    for q in range(4):
        cq = ct[q * Q : (q + 1) * Q]
        sc_t[q] = jnp.sum(cq * cq, axis=1, keepdims=True)
        pay_a[q] = cq[:, :128].astype(bf16)
        pay_b[q] = cq[:, 128:].astype(bf16)
    pl.semaphore_wait(barrier, len(peers))
    for c in (1, 0):
        for k in range(3):
            pay_copy(c, to(k), k).start()
    loads[1].wait()
    cs = lax.dot_general(hot[...], hs[...], (((1,), (1,)), ((), ())), preferred_element_type=f32)
    for q in range(4):
        cq = cs[q * Q : (q + 1) * Q]
        sq_s = jnp.sum(cq * cq, axis=1, keepdims=True)
        rest = jnp.concatenate([cq[:, 128:160], jnp.zeros((Q, 96), f32)], axis=1)
        rest = jnp.where(lane == 32, sc_t[q], jnp.where(lane == 33, sq_s, rest))
        rest = jnp.transpose(rest)
        tx[4 + q] = rest[32:40]
        pay_c[q, 0:128] = cq[:, :128].astype(bf16)
        pay_c[q, 128:160] = rest[:32].astype(bf16)
    for k in range(3):
        pay_copy(2, to(k), k).start()
    for k in range(3):
        tiny_copy(to(k), k).start()
    ends = []

    used = [3]

    def spread(buf, axis, at, number, rnd, value):
        buf[at] = value
        if axis == "g":
            devs = [sib]
        elif axis == "gx":
            devs = [{"group": 1 - g, "tok": (x + k) % 4} for k in (2, 1, 3)]
            devs += [at_axis("x", k) for k in (2, 1, 3)] + [sib]
        elif axis == "yz":
            devs = [at_plane(k) for k in PLANE]
        else:
            devs = [at_axis(axis, k) for k in (2, 1, 3)]
        cps = [pltpu.make_async_remote_copy(
            src_ref=buf.at[at], dst_ref=buf.at[at], send_sem=rnd_s.at[rnd], recv_sem=rnd_r.at[used[0] + n],
            device_id=d, device_id_type=MESH) for n, d in enumerate(devs)]
        used[0] += len(devs)
        for c in cps:
            c.start()
        ends.append((buf.at[0 : len(devs)], rnd_s.at[rnd]))

        def finish():
            for c in cps:
                c.wait_recv()
            return [buf[i] for i in range(number)]

        return finish

    def add_up(parts):
        total = parts[0]
        for p in parts[1:]:
            total = total + p
        return total

    def sums_x():
        for k in range(3):
            tiny_copy((x + 1) % 4, k).wait_recv()
        return add_up([tx[4 + x]] + [tx[(x + k) % 4] for k in (1, 2, 3)])

    small[1].wait()
    gain_t = tg[...].astype(f32)
    gain_s = sg[...].astype(f32).reshape(1, 160)
    eye = lax.broadcasted_iota(jnp.int32, (32, 32), 0) == lax.broadcasted_iota(jnp.int32, (32, 32), 1)
    gain_col = jnp.sum(jnp.where(eye, gain_s[:, 128:160], 0.0), axis=1, keepdims=True)

    def mine(c, lo, hi):
        own, others = pays[c]
        s = own[x, lo:hi].astype(f32)
        for k in (1, 2, 3):
            s = s + others[(x + k) % 4, lo:hi].astype(f32)
        return s

    def place(c):
        for k in range(3):
            pay_copy(c, to(k), k).wait_recv()
        if c == 0:
            xa[g, y, z, x, 0:128] = (mine(0, 0, 128) * gain_t[0:1]).astype(bf16)
        elif c == 1:
            xb[g, y, z, x] = (mine(1, 0, 128) * gain_t[1:2]).astype(bf16)
        else:
            xc[g, y, z, x, 0:128] = (mine(2, 0, 128) * gain_s[:, :128]).astype(bf16)
            rest = (mine(2, 128, 160) * gain_col).astype(bf16)
            xa[g, y, z, x, 128:144] = rest[:16]
            xc[g, y, z, x, 128:144] = rest[16:]

    order = ("xyz", "yzx", "zxy")
    here = {"x": x, "y": y, "z": z}
    everything = slice(None)

    def box(c, a1, a2, a3):
        if c == 0:
            return xa.at[g, a2, a3, a1]
        if c == 1:
            return xb.at[g, a1, a2, a3]
        return xc.at[g, a3, a1, a2]

    def coords(c):
        return [here[a] for a in order[c]]

    def ici(c, stage, n, ref, axis, k):
        return pltpu.make_async_remote_copy(
            src_ref=ref, dst_ref=ref, send_sem=ici_s.at[c, stage], recv_sem=ici_r.at[c, n],
            device_id=at_axis(axis, k), device_id_type=MESH)

    def sibling(c, n, ref):
        return pltpu.make_async_remote_copy(
            src_ref=ref, dst_ref=ref, send_sem=sib_s.at[c], recv_sem=sib_r.at[c, n],
            device_id=sib, device_id_type=MESH)

    def first(c, n):
        return ici(c, 0, n, box(c, *coords(c)), order[c][0], (2, 1, 3)[n])

    def second(c, n):
        a1, a2, a3 = coords(c)
        axis = order[c][1]
        if n == 0:
            return ici(c, 1, 4, box(c, everything, a2, a3), axis, 1)
        if n == 1:
            return ici(c, 1, 5, box(c, everything, a2, a3), axis, 3)
        if n == 2:
            return ici(c, 1, 6, box(c, pl.ds(0, 2), (a2 + 3) % 4, a3), axis, 1)
        return ici(c, 1, 7, box(c, pl.ds(2, 2), (a2 + 1) % 4, a3), axis, 3)

    def third(c, n, i):
        a1, a2, a3 = coords(c)
        axis = order[c][2]
        b2 = (a2 + off(i)) % 4
        if n == 0:
            return ici(c, 2, 8 + i, box(c, everything, b2, a3), axis, 1)
        if n == 1:
            return ici(c, 2, 12 + i, box(c, everything, b2, a3), axis, 3)
        if n == 2:
            return ici(c, 2, 16 + i, box(c, pl.ds(0, 2), b2, (a3 + 3) % 4), axis, 1)
        return ici(c, 2, 20 + i, box(c, pl.ds(2, 2), b2, (a3 + 1) % 4), axis, 3)

    def across(c, i, k):
        a1, a2, a3 = coords(c)
        return sibling(c, 4 * k + i, box(c, everything, (a2 + off(i)) % 4, (a3 + k) % 4))

    colors = (1, 2, 0)
    for c in colors:
        place(c)
        for n in range(3):
            first(c, n).start()
    finish = spread(tz, "z", z, 4, 1, sums_x())

    small[2].wait()
    digits = targets[...]
    table = jnp.concatenate(
        [(digits & 255), (digits >> 8) & 255, digits >> 16], axis=1).astype(f32).astype(bf16)
    first_entry = ((g * 4 + x) * 16 + v) * NV

    def find_targets(q, _):
        tok = tok_col[q].astype(jnp.int32)
        hot = jnp.where(
            (tok >> 7) == lax.broadcasted_iota(jnp.int32, (Q, 64), 1), 1.0, 0.0).astype(bf16)
        found = jnp.dot(hot, table, preferred_element_type=f32)
        mixed = found[:, :128] + 256.0 * found[:, 128:256] + 65536.0 * found[:, 256:]
        ids = jnp.sum(jnp.where(lane == (tok & 127), mixed, 0.0), axis=1, keepdims=True)
        tgt_col[q] = ids
        return 0

    acc_t[...] = jnp.zeros_like(acc_t)
    acc_s[...] = jnp.zeros_like(acc_s)

    for c in colors:
        for n in range(3):
            first(c, n).wait_recv()
        second(c, 0).start()
        second(c, 1).start()
    for c in colors:
        third(c, 0, 0).start()
        third(c, 1, 0).start()
        across(c, 0, 0).start()
    finish = spread(ty, "y", y, 4, 2, add_up(finish()))
    def near():
        for c in colors:
            second(c, 0).wait_recv()
            second(c, 2).start()
            second(c, 1).wait_recv()
            second(c, 3).start()
        for c in colors:
            third(c, 0, 1).start()
            third(c, 1, 1).start()
        for c in colors:
            for i in (1, 2):
                across(c, i, 0).start()

    def far():
        for c in colors:
            second(c, 2).wait_recv()
            second(c, 3).wait_recv()
            third(c, 0, 3).start()
            third(c, 1, 3).start()
            across(c, 3, 0).start()

    for c in loads[2:]:
        c.wait()

    def add(acc, xs, w, rows_of):
        xs = jnp.concatenate(xs, axis=1)

        ws_ = jnp.concatenate([w[r, :] for r in rows_of], axis=0)
        acc[...] = acc[...] + jnp.dot(xs, ws_, preferred_element_type=f32)

    def chunk(gg, yy, zz):
        return gg * 16 + yy * 4 + zz

    def rows_t(n, odd):
        return pl.ds(pl.multiple_of(n * 256 + 128 * odd, 128), 128)

    def multiply(i, ks):
        y_i = (y + off(i)) % 4
        z_i = (z + off(i)) % 4
        x_i = (x + off(i)) % 4
        both = (0, 1)
        at = [(gg, y_i, (z + k) % 4) for k in ks for gg in both]
        add(acc_t, [xa[gg, yy, zz, :, 0:128].reshape(ROWS, 128) for gg, yy, zz in at],
            wt, [rows_t(chunk(*a), 0) for a in at])
        for k in ks:
            xx = (x + k) % 4
            at = [(gg, yy, z_i) for gg in both for yy in range(4)]
            add(acc_t.at[pl.ds(pl.multiple_of(xx * Q, Q), Q)],
                [xb[gg, yy, zz, xx] for gg, yy, zz in at],
                wt, [rows_t(chunk(*a), 1) for a in at])
        at = [(gg, (y + k) % 4, zz) for k in ks for gg in both for zz in range(4)]
        add(acc_s.at[pl.ds(pl.multiple_of(x_i * Q, Q), Q)],
            [xc[gg, yy, zz, x_i, 0:128] for gg, yy, zz in at],
            ws, [pl.ds(pl.multiple_of(chunk(*a) * 160, 32), 128) for a in at])

    def multiply_rest(i):
        y_i = (y + off(i)) % 4
        x_i = (x + off(i)) % 4
        at = [(gg, y_i, zz) for gg in (0, 1) for zz in range(4)]
        xs = []
        for xx in range(4):
            t = jnp.concatenate([xa[gg, yy, zz, xx, 128:144] for gg, yy, zz in at], axis=0)
            xs.append(jnp.transpose(t.astype(f32)).astype(bf16))
        add(acc_s, [jnp.concatenate(xs, axis=0)], ws,
            [pl.ds(pl.multiple_of(chunk(*a) * 160 + 128, 16), 16) for a in at])
        xs = []
        rows_of = []
        for gg in (0, 1):
            for yp in (0, 2):
                at = [(gg, yy, zz) for yy in (yp, yp + 1) for zz in range(4)]
                t = jnp.concatenate([xc[gg, yy, zz, x_i, 128:144] for gg, yy, zz in at], axis=0)
                xs.append(jnp.transpose(t.astype(f32)).astype(bf16))
                rows_of += [pl.ds(pl.multiple_of(chunk(*a) * 160 + 144, 16), 16) for a in at]
        add(acc_s.at[pl.ds(pl.multiple_of(x_i * Q, Q), Q)], xs, ws, rows_of)

    def step(e, _):
        @pl.when(e < 4)
        def _():
            for c in colors:
                across(c, e, 0).wait_recv()
            multiply(e, (0,))

        @pl.when(e == 0)
        def _():
            lax.fori_loop(0, 4, find_targets, 0)
            near()

        @pl.when((e > 0) & (e < 5))
        def _():
            i = e - 1
            for c in colors:
                third(c, 0, i).wait_recv()
                third(c, 2, i).start()
                third(c, 1, i).wait_recv()
                third(c, 3, i).start()
            for c in colors:
                across(c, i, 3).start()
                across(c, i, 1).start()

        @pl.when(e == 1)
        def _():
            for c in colors:
                third(c, 0, 2).start()
                third(c, 1, 2).start()

        @pl.when(e == 1)
        def _():
            far()

        @pl.when((e > 1) & (e < 6))
        def _():
            i = e - 2
            for c in colors:
                for k in (1, 3):
                    across(c, i, k).wait_recv()
            multiply(i, (1, 3))

        @pl.when((e > 2) & (e < 7))
        def _():
            i = e - 3
            for c in colors:
                third(c, 2, i).wait_recv()
                third(c, 3, i).wait_recv()
                across(c, i, 2).start()

        @pl.when(e > 3)
        def _():
            i = e - 4
            for c in colors:
                across(c, i, 2).wait_recv()
            multiply(i, (2,))
            multiply_rest(i)

        return 0

    lax.fori_loop(0, 2, step, 0)
    finish = spread(tgp, "g", g, 2, 3, add_up(finish()))
    finish = spread(txx, "x", x, 4, 4, add_up(finish()))
    lax.fori_loop(2, 8, step, 0)

    parts = finish()
    width = jnp.where(lax.broadcasted_iota(jnp.int32, (8, 128), 0) % 2 == 0, float(DT), float(DS))
    scale = lax.rsqrt(jnp.concatenate([p[0:2] for p in parts], axis=0) / width + EPS)
    scale = jnp.transpose(jnp.concatenate([scale, jnp.zeros((120, 128), f32)], axis=0))
    for q in range(4):
        sc_t[q] = scale[:, 2 * q : 2 * q + 1]
        sc_s[q] = scale[:, 2 * q + 1 : 2 * q + 2]

    def stats(q, m):
        r = pl.ds(pl.multiple_of(q * Q, Q), Q)
        lt = acc_t[r, :] * sc_t[q]
        ls = acc_s[r, :] * sc_s[q]
        mt = jnp.max(lt, axis=1, keepdims=True)
        ms = jnp.max(ls, axis=1, keepdims=True)
        et = jnp.exp(lt - mt)
        zt = jnp.sum(et, axis=1, keepdims=True)
        dd = jnp.sum(et * (lt - ls), axis=1, keepdims=True)
        zs = jnp.sum(jnp.exp(ls - ms), axis=1, keepdims=True)
        col = tgt_col[q].astype(jnp.int32) - first_entry
        hit = col == lax.broadcasted_iota(jnp.int32, (Q, NV), 1)
        tl = jnp.sum(jnp.where(hit, ls, 0.0), axis=1, keepdims=True)
        for n, val in enumerate((mt + jnp.log(zt), ms + jnp.log(zs), dd / zt, tl)):
            m = jnp.where(lane == 4 * n + q, val, m)
        return m

    m = lax.fori_loop(0, 4, stats, jnp.zeros((Q, 128), f32))
    val = jnp.transpose(m)[:16]

    for axis, buf, at, number, rnd in (("gx", fx, 4 * g + x, 8, 5), ("yz", fy, v, 16, 6)):
        parts = spread(buf, axis, at, number, rnd, val)()

        def lse(lo):
            top = parts[0][lo : lo + 4]
            for p in parts[1:]:
                top = jnp.maximum(top, p[lo : lo + 4])
            es = [jnp.exp(p[lo : lo + 4] - top) for p in parts]
            tot = es[0]
            for e in es[1:]:
                tot = tot + e
            return top + jnp.log(tot), es, tot

        lse_t, es, tot = lse(0)
        lse_s, _, _ = lse(4)
        cross = es[0] * parts[0][8:12]
        tl = parts[0][12:16]
        for e, p in zip(es[1:], parts[1:]):
            cross = cross + e * p[8:12]
            tl = tl + p[12:16]
        val = jnp.concatenate([lse_t, lse_s, cross / tot, tl], axis=0)

    out[...] = val

    def left(ref, sem):
        pltpu.make_async_copy(ref, ref, sem).wait()

    left(tx.at[0:3], rnd_s.at[0])
    for ref, sem in ends:
        left(ref, sem)
    for c, ref in enumerate((xa, xb, xc)):
        left(pays[c][0].at[0:3], p1_s.at[c])
        left(ref.at[0, 0, 0, 0:3], ici_s.at[c, 0])
        left(ref.at[0, 0, 0:3], ici_s.at[c, 1])
        left(ref.at[0, 0:3], ici_s.at[c, 2])
        left(ref.at[0], sib_s.at[c])


def outputs(val_ref, counts, mask_time, out_kl, out_nll, out_loss):
    x = lax.axis_index("tok")
    lane256 = lax.broadcasted_iota(jnp.int32, (1, 256), 1)
    starts = []
    total = jnp.int32(0)
    for t in range(4):
        starts.append(total)
        total = total + counts[t]
    val = val_ref[...]
    lse_t, lse_s, cross, tl = (val[4 * n : 4 * n + 4] for n in range(4))
    kl = cross - lse_t + lse_s
    nll = lse_s - tl
    kl_total = jnp.sum(jnp.sum(kl, axis=1, keepdims=True), axis=0, keepdims=True)
    nll_total = jnp.sum(jnp.sum(nll, axis=1, keepdims=True), axis=0, keepdims=True)
    time = jnp.full((1, 1), mask_time[0], jnp.int32).astype(f32)
    masked = jnp.full((1, 1), total, jnp.int32).astype(f32)
    weight = 1000.0 / time
    out_loss[...] = jnp.concatenate([weight * nll_total / 8192.0, kl_total / masked], axis=1)

    cols = jnp.transpose(jnp.concatenate([kl, nll, jnp.zeros((120, 128), f32)], axis=0))
    start = jnp.int32(0)
    count = jnp.int32(0)
    for t in range(4):
        start = start + jnp.where(x == t, starts[t], 0)
        count = count + jnp.where(x == t, counts[t], 0)
    slot = lax.broadcasted_iota(jnp.int32, (Q, 256), 1)
    gap = lax.broadcasted_iota(jnp.int32, (Q, 256), 0) - slot
    for n, out in ((0, out_kl), (4, out_nll)):
        s = jnp.zeros((Q, 256), f32)
        for q in range(4):
            s = s + jnp.where(gap == start - q * Q, cols[:, n + q : n + q + 1], 0.0)
        s = jnp.sum(s, axis=0, keepdims=True)
        out[...] = jnp.where(lane256 < count, s, 0.0)


def shards(th, sh, tg, sg, wt, ws, targets, positions, counts, mask_time):
    vm = pl.BlockSpec(memory_space=pltpu.VMEM)
    sm = pl.BlockSpec(memory_space=pltpu.SMEM)
    anyspace = pl.BlockSpec(memory_space=pl.ANY)
    dma = pltpu.SemaphoreType.DMA
    val = pl.pallas_call(
        body,
        out_shape=jax.ShapeDtypeStruct((16, 128), f32),
        in_specs=[anyspace, anyspace, anyspace, vm, anyspace, anyspace, anyspace, anyspace, sm],
        out_specs=vm,
        scratch_shapes=[
            pltpu.VMEM((2048, 256), bf16),
            pltpu.VMEM((160, 2048), bf16),
            pltpu.VMEM((2, 128), bf16),
            pltpu.VMEM((64, 128), jnp.int32),
            pltpu.VMEM((8, 128), jnp.int32),
            pltpu.VMEM((ROWS, 2048), bf16),
            pltpu.VMEM((DT, NV), bf16),
            pltpu.VMEM((DS, NV), bf16),
            pltpu.VMEM((2, 4, 4, 4, XT, 128), bf16),
            pltpu.VMEM((2, 4, 4, 4, 128, 128), bf16),
            pltpu.VMEM((2, 4, 4, 4, XT, 128), bf16),
            pltpu.VMEM((ROWS, NV), f32),
            pltpu.VMEM((ROWS, NV), f32),
            pltpu.VMEM((4, Q, 1), f32),
            pltpu.VMEM((4, Q, 1), f32),
            pltpu.VMEM((4, Q, 1), f32),
            pltpu.VMEM((4, Q, 1), f32),
            pltpu.VMEM((4, 128, 128), bf16),
            pltpu.VMEM((4, 128, 128), bf16),
            pltpu.VMEM((4, 160, 128), bf16),
            pltpu.VMEM((4, 128, 128), bf16),
            pltpu.VMEM((4, 128, 128), bf16),
            pltpu.VMEM((4, 160, 128), bf16),
            pltpu.VMEM((8, 8, 128), f32),
            pltpu.VMEM((4, 8, 128), f32),
            pltpu.VMEM((4, 8, 128), f32),
            pltpu.VMEM((2, 8, 128), f32),
            pltpu.VMEM((4, 8, 128), f32),
            pltpu.VMEM((8, 16, 128), f32),
            pltpu.VMEM((16, 16, 128), f32),
            dma((13,)),
            dma((3,)),
            dma((3, 3)),
            dma((7,)),
            dma((35,)),
            dma((3, 3)),
            dma((3, N_ICI)),
            dma((3,)),
            dma((3, N_SIB)),
        ],
        compiler_params=pltpu.CompilerParams(
            collective_id=0, has_side_effects=True, vmem_limit_bytes=58 * 1024 * 1024),
        name="elbo",
    )(
        th, sh.T, tg.reshape(2, 128), sg, wt, ws,
        targets.reshape(64, 128), positions.reshape(8, 128), counts,
    )
    kl, nll, loss = pl.pallas_call(
        outputs,
        out_shape=(
            jax.ShapeDtypeStruct((1, 256), f32),
            jax.ShapeDtypeStruct((1, 256), f32),
            jax.ShapeDtypeStruct((1, 2), f32),
        ),
        in_specs=[vm, sm, sm],
        out_specs=(vm, vm, vm),
        name="slots",
    )(val, counts, mask_time)
    return kl.reshape(256), nll.reshape(256), loss.reshape(2)


def solution(mesh):
    feats = ("group", "vocab")
    cols = ("group", "tok", "vocab")
    in_specs = (
        P("tok", feats), P("tok", feats), P(feats), P(feats),
        P(None, cols), P(None, cols), P(), P(), P(), P(),
    )
    out_specs = (P("tok"), P("tok"), P())
    return jax.shard_map(shards, mesh=mesh, in_specs=in_specs, out_specs=out_specs, check_vma=False)
```

```python
import functools

import jax
import jax.numpy as jnp
from jax import lax
from jax.experimental import pallas as pl
from jax.experimental.pallas import tpu as pltpu
from jax.sharding import PartitionSpec as P

EPS = 1e-06
MESH = pl.DeviceIdType.MESH
f32 = jnp.float32
bf16 = jnp.bfloat16

ROWS = 512
PLANE = (10, 6, 14, 9, 11, 2, 8, 5, 7, 13, 15, 1, 3, 4, 12)
Q = 128
DT = 8192
DS = 5120
NV = 768
NT = 256
XT = 144

N_ICI = 24
N_SIB = 16


def off(i):
    return jnp.where(i < 2, i, 5 - i)


def body(
    th, sh, tg_any, sg, wt_hbm, ws_hbm, targets_any, positions_any, counts,
    out,
    ht, hs, tg, targets, positions, hot, wt, ws, xa, xb, xc, acc_t, acc_s, tok_col, tgt_col,
    sc_t, sc_s, pay_a, pay_b, pay_c, p1a, p1b, p1c, tx, tz, ty, txx, fx, fy,
    load_sem, p1_s, p1_r, rnd_s, rnd_r, ici_s, ici_r, sib_s, sib_r,
):
    g = lax.axis_index("group")
    x = lax.axis_index("tok")
    v = lax.axis_index("vocab")
    y = v // 4
    z = v % 4
    sib = {"group": 1 - g}

    def at_axis(axis, k):
        if axis == "x":
            return {"tok": (x + k) % 4}
        if axis == "y":
            return {"vocab": ((y + k) % 4) * 4 + z}
        return {"vocab": y * 4 + (z + k) % 4}

    def at_plane(k):
        return {"vocab": ((y + k // 4) % 4) * 4 + (z + k % 4) % 4}

    barrier = pltpu.get_barrier_semaphore()
    peers = [at_axis("x", k) for k in (1, 2, 3)] + [at_plane(k) for k in range(1, 16)] + [sib]
    peers += [{"group": 1 - g, "tok": (x + k) % 4} for k in (1, 2, 3)]
    small = [
        pltpu.make_async_copy(positions_any, positions, load_sem.at[10]),
        pltpu.make_async_copy(tg_any, tg, load_sem.at[11]),
        pltpu.make_async_copy(targets_any, targets, load_sem.at[12]),
    ]
    loads = [
        pltpu.make_async_copy(th, ht, load_sem.at[0]),
        pltpu.make_async_copy(sh, hs, load_sem.at[1]),
    ]
    for i in range(4):
        r = pl.ds(i * (DT // 4), DT // 4)
        loads.append(pltpu.make_async_copy(wt_hbm.at[r], wt.at[r], load_sem.at[2 + i]))
        r = pl.ds(i * (DS // 4), DS // 4)
        loads.append(pltpu.make_async_copy(ws_hbm.at[r], ws.at[r], load_sem.at[6 + i]))
    for c in small[:1] + loads[:2] + small[1:] + loads[2:]:
        c.start()
    for d in peers:
        pl.semaphore_signal(barrier, inc=1, device_id=d, device_id_type=MESH)

    starts = []
    total = jnp.int32(0)
    for t in range(4):
        starts.append(total)
        total = total + counts[t]
    lane256 = lax.broadcasted_iota(jnp.int32, (1, 256), 1)
    small[0].wait()
    pos_rows = []
    for t in range(4):
        p = jnp.concatenate([positions[2 * t : 2 * t + 1, :], positions[2 * t + 1 : 2 * t + 2, :]], axis=1)
        pos_rows.append(jnp.where(lane256 < counts[t], p + 2048 * t, 0))

    def tokens(q, _):
        d = (
            lax.broadcasted_iota(jnp.int32, (Q, 256), 0)
            + q * Q
            - lax.broadcasted_iota(jnp.int32, (Q, 256), 1)
        )
        s = jnp.zeros((Q, 256), jnp.int32)
        for t in range(4):
            s = s + jnp.where(d == starts[t], pos_rows[t], 0)
        tok_col[q] = jnp.sum(s.astype(f32), axis=1, keepdims=True)
        return 0

    lax.fori_loop(0, 4, tokens, 0)

    lane = lax.broadcasted_iota(jnp.int32, (Q, 128), 1)

    def tiny_copy(q, k):
        return pltpu.make_async_remote_copy(
            src_ref=tx.at[4 + q], dst_ref=tx.at[x], send_sem=rnd_s.at[0], recv_sem=rnd_r.at[k],
            device_id={"tok": q}, device_id_type=MESH)

    pays = ((pay_a, p1a), (pay_b, p1b), (pay_c, p1c))

    def pay_copy(c, q, k):
        src, dst = pays[c]
        return pltpu.make_async_remote_copy(
            src_ref=src.at[q], dst_ref=dst.at[x], send_sem=p1_s.at[c], recv_sem=p1_r.at[c, k],
            device_id={"tok": q}, device_id_type=MESH)

    def to(k):
        return (x + (2, 1, 3)[k]) % 4

    def make_hot(q, _):
        tok = tok_col[q].astype(jnp.int32) - 2048 * x
        hot[pl.ds(pl.multiple_of(q * Q, Q), Q), :] = jnp.where(
            tok == lax.broadcasted_iota(jnp.int32, (Q, 2048), 1), 1.0, 0.0).astype(bf16)
        return 0

    lax.fori_loop(0, 4, make_hot, 0)
    loads[0].wait()
    ct = jnp.dot(hot[...], ht[...], preferred_element_type=f32)
    for q in range(4):
        cq = ct[q * Q : (q + 1) * Q]
        pay_a[q] = cq[:, :128].astype(bf16)
        pay_b[q] = cq[:, 128:].astype(bf16)
    pl.semaphore_wait(barrier, len(peers))
    for c in (1, 0):
        for k in range(3):
            pay_copy(c, to(k), k).start()
    for q in range(4):
        ca, cb = pay_a[q].astype(f32), pay_b[q].astype(f32)
        sc_t[q] = jnp.sum(ca * ca + cb * cb, axis=1, keepdims=True)
    loads[1].wait()
    cs = lax.dot_general(hot[...], hs[...], (((1,), (1,)), ((), ())), preferred_element_type=f32)
    for q in range(4):
        cq = cs[q * Q : (q + 1) * Q]
        sq_s = jnp.sum(cq * cq, axis=1, keepdims=True)
        rest = jnp.concatenate([cq[:, 128:160], jnp.zeros((Q, 96), f32)], axis=1)
        rest = jnp.where(lane == 32, sc_t[q], jnp.where(lane == 33, sq_s, rest))
        rest = jnp.transpose(rest)
        tx[4 + q] = rest[32:40]
        pay_c[q, 0:128] = cq[:, :128].astype(bf16)
        pay_c[q, 128:160] = rest[:32].astype(bf16)
    for k in range(3):
        pay_copy(2, to(k), k).start()
    for k in range(3):
        tiny_copy(to(k), k).start()
    ends = []

    used = [3]

    def spread(buf, axis, at, number, rnd, value):
        buf[at] = value
        if axis == "gx":
            devs = [{"group": 1 - g, "tok": (x + k) % 4} for k in (2, 1, 3)]
            devs += [at_axis("x", k) for k in (2, 1, 3)] + [sib]
        elif axis == "yz":
            devs = [at_plane(k) for k in PLANE]
        else:
            devs = [at_axis(axis, k) for k in (2, 1, 3)]
        cps = [pltpu.make_async_remote_copy(
            src_ref=buf.at[at], dst_ref=buf.at[at], send_sem=rnd_s.at[rnd], recv_sem=rnd_r.at[used[0] + n],
            device_id=d, device_id_type=MESH) for n, d in enumerate(devs)]
        used[0] += len(devs)
        for c in cps:
            c.start()
        ends.append((buf.at[0 : len(devs)], rnd_s.at[rnd]))

        def finish():
            for c in cps:
                c.wait_recv()
            return [buf[i] for i in range(number)]

        return finish

    def add_up(parts):
        total = parts[0]
        for p in parts[1:]:
            total = total + p
        return total

    def sums_x():
        for k in range(3):
            tiny_copy((x + 1) % 4, k).wait_recv()
        return add_up([tx[4 + x]] + [tx[(x + k) % 4] for k in (1, 2, 3)])

    small[1].wait()
    gain_t = tg[...].astype(f32)
    gain_s = sg[...].astype(f32).reshape(1, 160)
    eye = lax.broadcasted_iota(jnp.int32, (32, 32), 0) == lax.broadcasted_iota(jnp.int32, (32, 32), 1)
    gain_col = jnp.sum(jnp.where(eye, gain_s[:, 128:160], 0.0), axis=1, keepdims=True)

    def mine(c, lo, hi):
        own, others = pays[c]
        s = own[x, lo:hi].astype(f32)
        for k in (1, 2, 3):
            s = s + others[(x + k) % 4, lo:hi].astype(f32)
        return s

    def place(c):
        for k in range(3):
            pay_copy(c, to(k), k).wait_recv()
        if c == 0:
            xa[g, y, z, x, 0:128] = (mine(0, 0, 128) * gain_t[0:1]).astype(bf16)
        elif c == 1:
            xb[g, y, z, x] = (mine(1, 0, 128) * gain_t[1:2]).astype(bf16)
        else:
            xc[g, y, z, x, 0:128] = (mine(2, 0, 128) * gain_s[:, :128]).astype(bf16)
            rest = (mine(2, 128, 160) * gain_col).astype(bf16)
            xa[g, y, z, x, 128:144] = rest[:16]
            xc[g, y, z, x, 128:144] = rest[16:]

    order = ("xyz", "yzx", "zxy")
    here = {"x": x, "y": y, "z": z}
    everything = slice(None)

    def box(c, a1, a2, a3):
        if c == 0:
            return xa.at[g, a2, a3, a1]
        if c == 1:
            return xb.at[g, a1, a2, a3]
        return xc.at[g, a3, a1, a2]

    def coords(c):
        return [here[a] for a in order[c]]

    def ici(c, stage, n, ref, axis, k):
        return pltpu.make_async_remote_copy(
            src_ref=ref, dst_ref=ref, send_sem=ici_s.at[c, stage], recv_sem=ici_r.at[c, n],
            device_id=at_axis(axis, k), device_id_type=MESH)

    def sibling(c, n, ref):
        return pltpu.make_async_remote_copy(
            src_ref=ref, dst_ref=ref, send_sem=sib_s.at[c], recv_sem=sib_r.at[c, n],
            device_id=sib, device_id_type=MESH)

    def first(c, n):
        return ici(c, 0, n, box(c, *coords(c)), order[c][0], (2, 1, 3)[n])

    def second(c, n):
        a1, a2, a3 = coords(c)
        axis = order[c][1]
        if n == 0:
            return ici(c, 1, 4, box(c, everything, a2, a3), axis, 1)
        if n == 1:
            return ici(c, 1, 5, box(c, everything, a2, a3), axis, 3)
        if n == 2:
            return ici(c, 1, 6, box(c, pl.ds(0, 2), (a2 + 3) % 4, a3), axis, 1)
        return ici(c, 1, 7, box(c, pl.ds(2, 2), (a2 + 1) % 4, a3), axis, 3)

    def third(c, n, i):
        a1, a2, a3 = coords(c)
        axis = order[c][2]
        b2 = (a2 + off(i)) % 4
        if n == 0:
            return ici(c, 2, 8 + i, box(c, everything, b2, a3), axis, 1)
        if n == 1:
            return ici(c, 2, 12 + i, box(c, everything, b2, a3), axis, 3)
        if n == 2:
            return ici(c, 2, 16 + i, box(c, pl.ds(0, 2), b2, (a3 + 3) % 4), axis, 1)
        return ici(c, 2, 20 + i, box(c, pl.ds(2, 2), b2, (a3 + 1) % 4), axis, 3)

    def across(c, i, k):
        a1, a2, a3 = coords(c)
        return sibling(c, 4 * k + i, box(c, everything, (a2 + off(i)) % 4, (a3 + k) % 4))

    colors = (1, 2, 0)
    for c in colors:
        place(c)
        for n in range(3):
            first(c, n).start()
    finish = spread(tz, "z", z, 4, 1, sums_x())

    small[2].wait()
    digits = targets[...]
    table = jnp.concatenate(
        [(digits & 255), (digits >> 8) & 255, digits >> 16], axis=1).astype(f32).astype(bf16)
    first_entry = ((g * 4 + x) * 16 + v) * NV

    def find_targets(q, _):
        tok = tok_col[q].astype(jnp.int32)
        hot = jnp.where(
            (tok >> 7) == lax.broadcasted_iota(jnp.int32, (Q, 64), 1), 1.0, 0.0).astype(bf16)
        found = jnp.dot(hot, table, preferred_element_type=f32)
        mixed = found[:, :128] + 256.0 * found[:, 128:256] + 65536.0 * found[:, 256:]
        ids = jnp.sum(jnp.where(lane == (tok & 127), mixed, 0.0), axis=1, keepdims=True)
        tgt_col[q] = ids
        return 0

    acc_t[...] = jnp.zeros_like(acc_t)
    acc_s[...] = jnp.zeros_like(acc_s)

    for c in colors:
        for n in range(3):
            first(c, n).wait_recv()
        second(c, 0).start()
        second(c, 1).start()
    for c in colors:
        third(c, 0, 0).start()
        third(c, 1, 0).start()
        across(c, 0, 0).start()
    finish = spread(ty, "y", y, 4, 2, add_up(finish()))
    def near():
        for c in colors:
            second(c, 0).wait_recv()
            second(c, 2).start()
            second(c, 1).wait_recv()
            second(c, 3).start()
        for c in colors:
            third(c, 0, 1).start()
            third(c, 1, 1).start()
        for c in colors:
            for i in (1, 2):
                across(c, i, 0).start()

    def far():
        for c in colors:
            second(c, 2).wait_recv()
            second(c, 3).wait_recv()
            third(c, 0, 3).start()
            third(c, 1, 3).start()
            across(c, 3, 0).start()

    for c in loads[2:]:
        c.wait()

    def add(acc, xs, w, rows_of):
        xs = jnp.concatenate(xs, axis=1)

        ws_ = jnp.concatenate([w[r, :] for r in rows_of], axis=0)
        acc[...] = acc[...] + jnp.dot(xs, ws_, preferred_element_type=f32)

    def chunk(gg, yy, zz):
        return gg * 16 + yy * 4 + zz

    def rows_t(n, odd):
        return pl.ds(pl.multiple_of(n * 256 + 128 * odd, 128), 128)

    def multiply(i, ks):
        y_i = (y + off(i)) % 4
        z_i = (z + off(i)) % 4
        x_i = (x + off(i)) % 4
        both = (0, 1)
        at = [(gg, y_i, (z + k) % 4) for k in ks for gg in both]
        add(acc_t, [xa[gg, yy, zz, :, 0:128].reshape(ROWS, 128) for gg, yy, zz in at],
            wt, [rows_t(chunk(*a), 0) for a in at])
        for k in ks:
            xx = (x + k) % 4
            at = [(gg, yy, z_i) for gg in both for yy in range(4)]
            add(acc_t.at[pl.ds(pl.multiple_of(xx * Q, Q), Q)],
                [xb[gg, yy, zz, xx] for gg, yy, zz in at],
                wt, [rows_t(chunk(*a), 1) for a in at])
        at = [(gg, (y + k) % 4, zz) for k in ks for gg in both for zz in range(4)]
        add(acc_s.at[pl.ds(pl.multiple_of(x_i * Q, Q), Q)],
            [xc[gg, yy, zz, x_i, 0:128] for gg, yy, zz in at],
            ws, [pl.ds(pl.multiple_of(chunk(*a) * 160, 32), 128) for a in at])

    def multiply_rest(i):
        y_i = (y + off(i)) % 4
        x_i = (x + off(i)) % 4
        at = [(gg, y_i, zz) for gg in (0, 1) for zz in range(4)]
        xs = []
        for xx in range(4):
            t = jnp.concatenate([xa[gg, yy, zz, xx, 128:144] for gg, yy, zz in at], axis=0)
            xs.append(jnp.transpose(t.astype(f32)).astype(bf16))
        add(acc_s, [jnp.concatenate(xs, axis=0)], ws,
            [pl.ds(pl.multiple_of(chunk(*a) * 160 + 128, 16), 16) for a in at])
        xs = []
        rows_of = []
        for gg in (0, 1):
            for yp in (0, 2):
                at = [(gg, yy, zz) for yy in (yp, yp + 1) for zz in range(4)]
                t = jnp.concatenate([xc[gg, yy, zz, x_i, 128:144] for gg, yy, zz in at], axis=0)
                xs.append(jnp.transpose(t.astype(f32)).astype(bf16))
                rows_of += [pl.ds(pl.multiple_of(chunk(*a) * 160 + 144, 16), 16) for a in at]
        add(acc_s.at[pl.ds(pl.multiple_of(x_i * Q, Q), Q)], xs, ws, rows_of)

    def step(e, _):
        @pl.when(e < 4)
        def _():
            for c in colors:
                across(c, e, 0).wait_recv()
            multiply(e, (0,))

        @pl.when(e == 0)
        def _():
            lax.fori_loop(0, 4, find_targets, 0)
            near()

        @pl.when((e > 0) & (e < 5))
        def _():
            i = e - 1
            for c in colors:
                third(c, 0, i).wait_recv()
                third(c, 2, i).start()
                third(c, 1, i).wait_recv()
                third(c, 3, i).start()
            for c in colors:
                across(c, i, 3).start()
                across(c, i, 1).start()

        @pl.when(e == 1)
        def _():
            for c in colors:
                third(c, 0, 2).start()
                third(c, 1, 2).start()

        @pl.when(e == 1)
        def _():
            far()

        @pl.when((e > 1) & (e < 6))
        def _():
            i = e - 2
            for c in colors:
                for k in (1, 3):
                    across(c, i, k).wait_recv()
            multiply(i, (1, 3))

        @pl.when((e > 2) & (e < 7))
        def _():
            i = e - 3
            for c in colors:
                third(c, 2, i).wait_recv()
                third(c, 3, i).wait_recv()
                across(c, i, 2).start()

        @pl.when(e > 3)
        def _():
            i = e - 4
            for c in colors:
                across(c, i, 2).wait_recv()
            multiply(i, (2,))
            multiply_rest(i)

        return 0

    lax.fori_loop(0, 2, step, 0)
    finish = spread(txx, "gx", 4 * g + x, 8, 3, add_up(finish()))
    lax.fori_loop(2, 8, step, 0)

    parts = finish()
    parts = [parts[i] + parts[4 + i] for i in range(4)]
    width = jnp.where(lax.broadcasted_iota(jnp.int32, (8, 128), 0) % 2 == 0, float(DT), float(DS))
    scale = lax.rsqrt(jnp.concatenate([p[0:2] for p in parts], axis=0) / width + EPS)
    scale = jnp.transpose(jnp.concatenate([scale, jnp.zeros((120, 128), f32)], axis=0))
    for q in range(4):
        sc_t[q] = scale[:, 2 * q : 2 * q + 1]
        sc_s[q] = scale[:, 2 * q + 1 : 2 * q + 2]

    def stats(q, m):
        r = pl.ds(pl.multiple_of(q * Q, Q), Q)
        lt = acc_t[r, :] * sc_t[q]
        ls = acc_s[r, :] * sc_s[q]
        mt = jnp.max(lt, axis=1, keepdims=True)
        ms = jnp.max(ls, axis=1, keepdims=True)
        et = jnp.exp(lt - mt)
        zt = jnp.sum(et, axis=1, keepdims=True)
        dd = jnp.sum(et * (lt - ls), axis=1, keepdims=True)
        zs = jnp.sum(jnp.exp(ls - ms), axis=1, keepdims=True)
        col = tgt_col[q].astype(jnp.int32) - first_entry
        hit = col == lax.broadcasted_iota(jnp.int32, (Q, NV), 1)
        tl = jnp.sum(jnp.where(hit, ls, 0.0), axis=1, keepdims=True)
        for n, val in enumerate((mt + jnp.log(zt), ms + jnp.log(zs), dd / zt, tl)):
            m = jnp.where(lane == 4 * n + q, val, m)
        return m

    m = lax.fori_loop(0, 4, stats, jnp.zeros((Q, 128), f32))
    val = jnp.transpose(m)[:16]

    for axis, buf, at, number, rnd in (("gx", fx, 4 * g + x, 8, 5), ("yz", fy, v, 16, 6)):
        parts = spread(buf, axis, at, number, rnd, val)()

        def lse(lo):
            top = parts[0][lo : lo + 4]
            for p in parts[1:]:
                top = jnp.maximum(top, p[lo : lo + 4])
            es = [jnp.exp(p[lo : lo + 4] - top) for p in parts]
            tot = es[0]
            for e in es[1:]:
                tot = tot + e
            return top + jnp.log(tot), es, tot

        lse_t, es, tot = lse(0)
        lse_s, _, _ = lse(4)
        cross = es[0] * parts[0][8:12]
        tl = parts[0][12:16]
        for e, p in zip(es[1:], parts[1:]):
            cross = cross + e * p[8:12]
            tl = tl + p[12:16]
        val = jnp.concatenate([lse_t, lse_s, cross / tot, tl], axis=0)

    out[...] = val

    def left(ref, sem):
        pltpu.make_async_copy(ref, ref, sem).wait()

    left(tx.at[0:3], rnd_s.at[0])
    for ref, sem in ends:
        left(ref, sem)
    for c, ref in enumerate((xa, xb, xc)):
        left(pays[c][0].at[0:3], p1_s.at[c])
        left(ref.at[0, 0, 0, 0:3], ici_s.at[c, 0])
        left(ref.at[0, 0, 0:3], ici_s.at[c, 1])
        left(ref.at[0, 0:3], ici_s.at[c, 2])
        left(ref.at[0], sib_s.at[c])


def outputs(val_ref, counts, mask_time, out_kl, out_nll, out_loss):
    x = lax.axis_index("tok")
    lane256 = lax.broadcasted_iota(jnp.int32, (1, 256), 1)
    starts = []
    total = jnp.int32(0)
    for t in range(4):
        starts.append(total)
        total = total + counts[t]
    val = val_ref[...]
    lse_t, lse_s, cross, tl = (val[4 * n : 4 * n + 4] for n in range(4))
    kl = cross - lse_t + lse_s
    nll = lse_s - tl
    kl_total = jnp.sum(jnp.sum(kl, axis=1, keepdims=True), axis=0, keepdims=True)
    nll_total = jnp.sum(jnp.sum(nll, axis=1, keepdims=True), axis=0, keepdims=True)
    time = jnp.full((1, 1), mask_time[0], jnp.int32).astype(f32)
    masked = jnp.full((1, 1), total, jnp.int32).astype(f32)
    weight = 1000.0 / time
    out_loss[...] = jnp.concatenate([weight * nll_total / 8192.0, kl_total / masked], axis=1)

    cols = jnp.transpose(jnp.concatenate([kl, nll, jnp.zeros((120, 128), f32)], axis=0))
    start = jnp.int32(0)
    count = jnp.int32(0)
    for t in range(4):
        start = start + jnp.where(x == t, starts[t], 0)
        count = count + jnp.where(x == t, counts[t], 0)
    slot = lax.broadcasted_iota(jnp.int32, (Q, 256), 1)
    gap = lax.broadcasted_iota(jnp.int32, (Q, 256), 0) - slot
    for n, out in ((0, out_kl), (4, out_nll)):
        s = jnp.zeros((Q, 256), f32)
        for q in range(4):
            s = s + jnp.where(gap == start - q * Q, cols[:, n + q : n + q + 1], 0.0)
        s = jnp.sum(s, axis=0, keepdims=True)
        out[...] = jnp.where(lane256 < count, s, 0.0)


def shards(th, sh, tg, sg, wt, ws, targets, positions, counts, mask_time):
    vm = pl.BlockSpec(memory_space=pltpu.VMEM)
    sm = pl.BlockSpec(memory_space=pltpu.SMEM)
    anyspace = pl.BlockSpec(memory_space=pl.ANY)
    dma = pltpu.SemaphoreType.DMA
    val = pl.pallas_call(
        body,
        out_shape=jax.ShapeDtypeStruct((16, 128), f32),
        in_specs=[anyspace, anyspace, anyspace, vm, anyspace, anyspace, anyspace, anyspace, sm],
        out_specs=vm,
        scratch_shapes=[
            pltpu.VMEM((2048, 256), bf16),
            pltpu.VMEM((160, 2048), bf16),
            pltpu.VMEM((2, 128), bf16),
            pltpu.VMEM((64, 128), jnp.int32),
            pltpu.VMEM((8, 128), jnp.int32),
            pltpu.VMEM((ROWS, 2048), bf16),
            pltpu.VMEM((DT, NV), bf16),
            pltpu.VMEM((DS, NV), bf16),
            pltpu.VMEM((2, 4, 4, 4, XT, 128), bf16),
            pltpu.VMEM((2, 4, 4, 4, 128, 128), bf16),
            pltpu.VMEM((2, 4, 4, 4, XT, 128), bf16),
            pltpu.VMEM((ROWS, NV), f32),
            pltpu.VMEM((ROWS, NV), f32),
            pltpu.VMEM((4, Q, 1), f32),
            pltpu.VMEM((4, Q, 1), f32),
            pltpu.VMEM((4, Q, 1), f32),
            pltpu.VMEM((4, Q, 1), f32),
            pltpu.VMEM((4, 128, 128), bf16),
            pltpu.VMEM((4, 128, 128), bf16),
            pltpu.VMEM((4, 160, 128), bf16),
            pltpu.VMEM((4, 128, 128), bf16),
            pltpu.VMEM((4, 128, 128), bf16),
            pltpu.VMEM((4, 160, 128), bf16),
            pltpu.VMEM((8, 8, 128), f32),
            pltpu.VMEM((4, 8, 128), f32),
            pltpu.VMEM((4, 8, 128), f32),
            pltpu.VMEM((8, 8, 128), f32),
            pltpu.VMEM((8, 16, 128), f32),
            pltpu.VMEM((16, 16, 128), f32),
            dma((13,)),
            dma((3,)),
            dma((3, 3)),
            dma((7,)),
            dma((38,)),
            dma((3, 3)),
            dma((3, N_ICI)),
            dma((3,)),
            dma((3, N_SIB)),
        ],
        compiler_params=pltpu.CompilerParams(
            collective_id=0, has_side_effects=True, vmem_limit_bytes=58 * 1024 * 1024),
        name="elbo",
    )(
        th, sh.T, tg.reshape(2, 128), sg, wt, ws,
        targets.reshape(64, 128), positions.reshape(8, 128), counts,
    )
    kl, nll, loss = pl.pallas_call(
        outputs,
        out_shape=(
            jax.ShapeDtypeStruct((1, 256), f32),
            jax.ShapeDtypeStruct((1, 256), f32),
            jax.ShapeDtypeStruct((1, 2), f32),
        ),
        in_specs=[vm, sm, sm],
        out_specs=(vm, vm, vm),
        name="slots",
    )(val, counts, mask_time)
    return kl.reshape(256), nll.reshape(256), loss.reshape(2)


def solution(mesh):
    feats = ("group", "vocab")
    cols = ("group", "tok", "vocab")
    in_specs = (
        P("tok", feats), P("tok", feats), P(feats), P(feats),
        P(None, cols), P(None, cols), P(), P(), P(), P(),
    )
    out_specs = (P("tok"), P("tok"), P())
    return jax.shard_map(shards, mesh=mesh, in_specs=in_specs, out_specs=out_specs, check_vma=False)
```
